32 devices in a mesh: gx: 2 (over x), gy: 4 (over z), gz: 4 (over y, core).
Axes of the slice: x: 2, y: 2, z: 4, core: 2. Of those that a mesh axis runs over, the one named last changes fastest.
Arguments:
- pressure: float32 [2, 32, 32, 512], P(None, 'gx', 'gy', 'gz'), may hold values from -6 to 6
- saturation: float32 [3, 2, 32, 32, 512], P(None, None, 'gx', 'gy', 'gz'), may hold values from 0.15 to 0.45
- permeability: float32 [32, 32, 512], P('gx', 'gy', 'gz'), may hold values from 0.5 to 2
- porosity: float32 [32, 32, 512], P('gx', 'gy', 'gz'), may hold values from 0.1 to 0.35
- upwind_flags: int32 [32, 32, 512], P('gx', 'gy', 'gz'), may hold values from 0 to 63
- diag_inverse: float32 [2, 3, 3, 32, 32, 512], P(None, None, None, 'gx', 'gy', 'gz'), may hold values from -0.12 to 0.8, as said below
- seismic_obs: float32 [32, 32, 512], P('gx', 'gy', 'gz'), may hold values from -6 to 6
- well_x: int32 [2, 4, 64], P('gx', 'gy'), may hold values from 0 to 15
- well_y: int32 [2, 4, 64], P('gx', 'gy'), may hold values from 0 to 7
- well_top: int32 [2, 4, 64], P('gx', 'gy'), may hold values from 0 to 255
- well_len: int32 [2, 4, 64], P('gx', 'gy'), may hold values from 128 to 256
- well_bhp: float32 [2, 2, 4, 64], P(None, 'gx', 'gy'), may hold values from -3 to 3
- well_obs: float32 [2, 2, 4, 64], P(None, 'gx', 'gy'), may hold values from -48 to 48
- fault_cell: int32 [32, 16, 128], P(('gx', 'gy', 'gz')), may hold values from 0 to 16383
- fault_count: int32 [32, 16], P(('gx', 'gy', 'gz')), may hold values from 0 to 128, as said below
- fault_trans: float32 [32, 16, 128], P(('gx', 'gy', 'gz')), may hold values from 0.5 to 2, as said below
- fault_up: int32 [32, 16, 128], P(('gx', 'gy', 'gz')), may hold values from 0 to 3, as said below
- region_map: int32 [8, 8, 128], P('gx', 'gy', 'gz'), may hold values from 0 to 1023
Outputs:
- adjoint: float32 [2, 3, 32, 32, 512], P(None, None, 'gx', 'gy', 'gz')
- region_grad: float32 [2, 1024], P(None, ('gx', 'gy', 'gz'))
The draws below stay inside these ranges and needn't reach their ends.
Inputs may be any that keep to these rules, and one draw needn't show every extreme that they name: fault_count[dev][p] equals fault_count[i * 16 + p][a] of the connection's other end; a device has no connections with itself; in every draw one device of each group of 16 has exactly 128 connections with every other device of its group. `fault_cell`: slot s of dev toward peer p and slot s of that peer toward dev are the two ends of one connection. `fault_trans`: both ends of a connection hold the same transmissibility. `fault_up`: the two ends of a connection hold opposite bits. `diag_inverse`: entries [t][0][0] lie in 0.25 to 0.5, entries [t][u][u] for u = 1, 2 in 0.4 to 0.8, all others in -0.12 to 0.12.
All inputs are finite; a program needn't handle non-finite values.
Results may differ from the reference program's by a relative error of at most 0.0001.
Values sent between devices are 32-bit elements; how exact they have to be, the bound alone decides.
A program may use at most 128 MiB of HBM per device.

```python
import math
import jax
import jax.numpy as jnp
from jax import lax

CX = 16
CY = 8
CZ = 128
ITERS = 6
WELL_COL = 64
CAP = 128
BOX = 4
GROUPS = 2
PEERS = 16
NX = 32
NY = 32
NZ = 512
NREG = 1024
N_GX = 2
N_GY = 4
N_GZ = 4
DEVICES = 32


def symmetric_pick(base_draw):
    members = jnp.arange(PEERS)
    lower_index = jnp.minimum(members[:, None], members[None, :])
    upper_index = jnp.maximum(members[:, None], members[None, :])
    return base_draw[:, lower_index, upper_index]


def draw_fault_count(key, part):
    base_draw = jax.random.randint(jax.random.fold_in(key, 101), (GROUPS, PEERS, PEERS), 0, CAP // 2 + 1)
    paired = symmetric_pick(base_draw)
    busiest = jax.random.randint(jax.random.fold_in(key, 102), (GROUPS,), 0, PEERS)
    members = jnp.arange(PEERS)
    touches = (members[None, :, None] == busiest[:, None, None]) | (members[None, None, :] == busiest[:, None, None])
    paired = jnp.where(touches, CAP, paired)
    paired = jnp.where((members[:, None] == members[None, :])[None], 0, paired)
    return paired.reshape(GROUPS * PEERS, PEERS).astype(jnp.int32)


def draw_fault_trans(key, part):
    uniform_draw = jax.random.uniform(jax.random.fold_in(key, 103), (GROUPS, PEERS, PEERS, CAP), jnp.float32)
    values = 0.5 + 1.5 * uniform_draw
    return symmetric_pick(values).reshape(GROUPS * PEERS, PEERS, CAP).astype(jnp.float32)


def draw_fault_up(key, part):
    base_draw = jax.random.randint(jax.random.fold_in(key, 104), (GROUPS, PEERS, PEERS, CAP), 0, 4)
    paired = symmetric_pick(base_draw)
    members = jnp.arange(PEERS)
    flipped = (members[:, None] > members[None, :])[None, :, :, None]
    return jnp.where(flipped, 3 - paired, paired).reshape(GROUPS * PEERS, PEERS, CAP).astype(jnp.int32)


def draw_diag_inverse(key, part):
    uniform_draw = jax.random.uniform(jax.random.fold_in(key, 105), (2, 3, 3, NX, NY, NZ), jnp.float32)
    lower_table = jnp.array([[0.25, -0.12, -0.12], [-0.12, 0.4, -0.12], [-0.12, -0.12, 0.4]], jnp.float32)
    width_table = jnp.array([[0.25, 0.24, 0.24], [0.24, 0.4, 0.24], [0.24, 0.24, 0.4]], jnp.float32)
    result = lower_table[None, :, :, None, None, None] + width_table[None, :, :, None, None, None] * uniform_draw
    return result.astype(jnp.float32)


def place_ends(values, key, low, high):
    longest = values.shape.index(max(values.shape))
    spots = []
    for shift in (0, 1):
        where = [jax.random.randint(jax.random.fold_in(key, axis), (), 0, length) for axis, length in enumerate(values.shape)]
        where[longest] = (where[longest] + shift) % values.shape[longest]
        spots.append(tuple(where))
    return values.at[spots[0]].set(low).at[spots[1]].set(high)


def levels(key, dims, cuts, low, top_value):
    def one(position, parts):
        draws = jax.random.uniform(jax.random.fold_in(jax.random.fold_in(key, 6), position), (parts,), jnp.float32, low / len(cuts), top_value / len(cuts))
        return jnp.repeat(jnp.exp(draws), dims[position] // parts).reshape((-1,) + (1,) * (len(dims) - position - 1))

    factor_of = one(*cuts[0])
    for cut in cuts[1:]:
        factor_of = factor_of * one(*cut)
    return factor_of


def scatter_about(rng, dims, deviation, most, cuts=(), held_as=jnp.bfloat16):
    values = deviation * jax.random.normal(rng, dims, jnp.float32)
    if cuts:
        values = values * levels(rng, dims, cuts, -0.22, 0.18)
    return jnp.clip(values, -most, most).astype(held_as)


def setup_inputs(seed: int = 0) -> dict:
    splits = jax.random.split(jax.random.key(seed), 19)
    return {
        "pressure": scatter_about(splits[0], (2, NX, NY, NZ), 1.0, 6.0, ((1, 2), (2, 4), (3, 4)), jnp.float32),
        "saturation": jnp.clip(0.15 + 0.29999998 * jax.random.uniform(splits[1], (3, 2, NX, NY, NZ), jnp.float32) ** levels(splits[1], (3, 2, NX, NY, NZ), ((2, 2), (3, 4), (4, 4)), -0.2, 0.2), 0.15, 0.45),
        "permeability": jnp.clip(jnp.exp(math.log(2.0) - 1.3862944 * jax.random.uniform(splits[2], (NX, NY, NZ), jnp.float32) ** levels(splits[2], (NX, NY, NZ), ((0, 2), (1, 4), (2, 4)), -0.2, 0.2)), 0.5, 2.0),
        "porosity": jnp.clip(0.1 + 0.25 * jax.random.uniform(splits[3], (NX, NY, NZ), jnp.float32) ** levels(splits[3], (NX, NY, NZ), ((0, 2), (1, 4), (2, 4)), -0.2, 0.2), 0.1, 0.35),
        "upwind_flags": place_ends(jax.random.randint(splits[4], (NX, NY, NZ), 0, 64), jax.random.fold_in(splits[4], 1), 0, 63).astype(jnp.int32),
        "diag_inverse": draw_diag_inverse(jax.random.fold_in(splits[18], 71), 0),
        "seismic_obs": scatter_about(splits[6], (NX, NY, NZ), 1.0, 6.0, ((0, 2), (1, 4), (2, 4)), jnp.float32),
        "well_x": place_ends(jax.random.randint(splits[7], (N_GX, N_GY, WELL_COL), 0, CX), jax.random.fold_in(splits[7], 1), 0, CX - 1).astype(jnp.int32),
        "well_y": place_ends(jax.random.randint(splits[8], (N_GX, N_GY, WELL_COL), 0, CY), jax.random.fold_in(splits[8], 1), 0, CY - 1).astype(jnp.int32),
        "well_top": place_ends(jax.random.randint(splits[9], (N_GX, N_GY, WELL_COL), 0, NZ // 2), jax.random.fold_in(splits[9], 1), 0, (NZ // 2) - 1).astype(jnp.int32),
        "well_len": place_ends(jax.random.randint(splits[10], (N_GX, N_GY, WELL_COL), NZ // 4, NZ // 2 + 1), jax.random.fold_in(splits[10], 1), NZ // 4, (NZ // 2 + 1) - 1).astype(jnp.int32),
        "well_bhp": scatter_about(splits[11], (2, N_GX, N_GY, WELL_COL), 0.5, 3.0, ((1, 2), (2, 4)), jnp.float32),
        "well_obs": scatter_about(splits[12], (2, N_GX, N_GY, WELL_COL), 8.0, 48.0, ((1, 2), (2, 4)), jnp.float32),
        "fault_cell": place_ends(jax.random.randint(splits[13], (DEVICES, PEERS, CAP), 0, CX * CY * CZ), jax.random.fold_in(splits[13], 1), 0, (CX * CY * CZ) - 1).astype(jnp.int32),
        "fault_count": draw_fault_count(jax.random.fold_in(splits[18], 71), 0),
        "fault_trans": draw_fault_trans(jax.random.fold_in(splits[18], 71), 0),
        "fault_up": draw_fault_up(jax.random.fold_in(splits[18], 71), 0),
        "region_map": place_ends(jax.random.randint(splits[17], (NX // BOX, NY // BOX, NZ // BOX), 0, NREG), jax.random.fold_in(splits[17], 1), 0, NREG - 1).astype(jnp.int32),
    }


fluid_viscosity = (0.4, 0.5, 1.0)
sigma_sq = 64.0

def phase_mobility(water_sat, oil_sat):
    gas_sat = 1.0 - water_sat - oil_sat
    return jnp.stack([water_sat * water_sat / fluid_viscosity[0], oil_sat * oil_sat / fluid_viscosity[1], gas_sat * gas_sat / fluid_viscosity[2]])

def mobility_slopes(water_sat, oil_sat):
    gas_sat = 1.0 - water_sat - oil_sat
    return (2.0 * water_sat / fluid_viscosity[0] - 2.0 * gas_sat / fluid_viscosity[2], 2.0 * oil_sat / fluid_viscosity[1] - 2.0 * gas_sat / fluid_viscosity[2])

def shift_ahead(quantity, along_axis):
    extent = quantity.shape[along_axis]
    border = jnp.zeros_like(lax.slice_in_dim(quantity, 0, 1, axis=along_axis))
    return lax.slice_in_dim(jnp.concatenate([quantity, border], axis=along_axis), 1, extent + 1, axis=along_axis)

def shift_behind(quantity, along_axis):
    extent = quantity.shape[along_axis]
    border = jnp.zeros_like(lax.slice_in_dim(quantity, 0, 1, axis=along_axis))
    return lax.slice_in_dim(jnp.concatenate([border, quantity], axis=along_axis), 0, extent, axis=along_axis)

def face_coefficients(permeability, mobility, upwind_flags, step_index):
    ahead_list = []
    behind_list = []
    for direction in range(3):
        face_trans = jnp.sqrt(permeability * shift_ahead(permeability, direction))
        upwind_bit = jnp.bitwise_and(jnp.right_shift(upwind_flags, 3 * step_index + direction), 1)
        chosen = jnp.where(upwind_bit[None] == 1, mobility, shift_ahead(mobility, direction + 1))
        coefficient = face_trans[None] * chosen
        ahead_list.append(coefficient)
        behind_list.append(shift_behind(coefficient, direction + 1))
    return (ahead_list, behind_list)

def global_cells(device_ids, cell_index):
    block_x = device_ids // PEERS
    block_y = device_ids // N_GZ % N_GY
    block_z = device_ids % N_GZ
    local_x = cell_index // (CY * CZ)
    local_y = cell_index // CZ % CY
    local_z = cell_index % CZ
    return ((block_x * CX + local_x) * NY + block_y * CY + local_y) * NZ + block_z * CZ + local_z

def apply_inverse(inverse, residual):
    return lax.optimization_barrier(jnp.sum(inverse * residual[:, None], axis=0))

def neighbour_sum(lagrange, ahead_list, behind_list, fault_coef, own_cells, other_cells):
    upper_terms = [lax.optimization_barrier(jnp.sum(ahead_list[direction] * shift_ahead(lagrange, direction + 1), axis=0)) for direction in range(3)]
    lower_terms = [lax.optimization_barrier(jnp.sum(behind_list[direction] * shift_behind(lagrange, direction + 1), axis=0)) for direction in range(3)]
    face_total = upper_terms[0] + lower_terms[0] + upper_terms[1] + lower_terms[1] + upper_terms[2] + lower_terms[2]
    flattened = lagrange.reshape(3, -1)
    contribution = lax.optimization_barrier(jnp.sum(fault_coef * flattened[:, other_cells], axis=0))
    faults = jnp.zeros((flattened.shape[1],), jnp.float32).at[own_cells.reshape(-1)].add(contribution.reshape(-1))
    return face_total + faults.reshape(lagrange.shape[1:])

def box_sums(quantity):
    shaped = quantity.reshape(quantity.shape[0] // BOX, BOX, quantity.shape[1] // BOX, BOX, quantity.shape[2] // BOX, BOX)
    return lax.optimization_barrier(jnp.sum(shaped, axis=(1, 3, 5))).reshape(-1)

def reference(pressure, saturation, permeability, porosity, upwind_flags, diag_inverse, seismic_obs, well_x, well_y, well_top, well_len, well_bhp, well_obs, fault_cell, fault_count, fault_trans, fault_up, region_map):
    mobility = [phase_mobility(saturation[step_index + 1, 0], saturation[step_index + 1, 1]) for step_index in range(2)]
    coefficients = [face_coefficients(permeability, mobility[step_index], upwind_flags, step_index) for step_index in range(2)]
    devices = GROUPS * PEERS
    device_ids = jnp.arange(devices, dtype=jnp.int32)[:, None, None]
    peer_index = jnp.arange(PEERS, dtype=jnp.int32)[None, :, None]
    peer_devices = device_ids // PEERS * PEERS + peer_index
    peer_cells = jnp.transpose(fault_cell.reshape(GROUPS, PEERS, PEERS, CAP), (0, 2, 1, 3)).reshape(devices, PEERS, CAP)
    own_cells = global_cells(device_ids, fault_cell)
    other_cells = global_cells(peer_devices, peer_cells)
    live_slots = (jnp.arange(CAP, dtype=jnp.int32)[None, None, :] < fault_count[:, :, None]).astype(jnp.float32)
    fault_coef = []
    for step_index in range(2):
        flattened = mobility[step_index].reshape(3, -1)
        upwind_bit = jnp.bitwise_and(jnp.right_shift(fault_up, step_index), 1)
        chosen = jnp.where(upwind_bit[None] == 1, flattened[:, own_cells], flattened[:, other_cells])
        fault_coef.append(fault_trans[None] * chosen * live_slots[None])
    column_x = (jnp.arange(N_GX, dtype=jnp.int32)[:, None, None] * CX + well_x).reshape(-1)
    column_y = (jnp.arange(N_GY, dtype=jnp.int32)[None, :, None] * CY + well_y).reshape(-1)
    top_cells = well_top.reshape(-1)[:, None]
    depth_index = jnp.arange(NZ, dtype=jnp.int32)[None, :]
    perforated = ((depth_index >= top_cells) & (depth_index < top_cells + well_len.reshape(-1)[:, None])).astype(jnp.float32)
    column_perm = permeability[column_x, column_y]
    sources = []
    explicit = jnp.zeros(permeability.shape, jnp.float32)
    for step_index in range(2):
        column_pressure = pressure[step_index][column_x, column_y]
        column_total = lax.optimization_barrier(jnp.sum(mobility[step_index][:, column_x, column_y], axis=0))
        drawdown = column_pressure - well_bhp[step_index].reshape(-1)[:, None]
        well_rate = lax.optimization_barrier(jnp.sum(perforated * column_perm * column_total * drawdown, axis=1))
        misfit = (well_rate - well_obs[step_index].reshape(-1)) / sigma_sq
        water_slope, oil_slope = mobility_slopes(saturation[step_index + 1, 0][column_x, column_y], saturation[step_index + 1, 1][column_x, column_y])
        weight = misfit[:, None] * column_perm * perforated
        added = jnp.stack([weight * column_total, weight * drawdown * water_slope, weight * drawdown * oil_slope])
        sources.append(jnp.zeros((3,) + permeability.shape, jnp.float32).at[:, column_x, column_y].add(added))
        explicit = explicit.at[column_x, column_y].add(weight * column_total * drawdown)
    sources[1] = sources[1].at[1].add(saturation[2, 0] - seismic_obs)

    def solve(step_index, source):
        ahead_list, behind_list = coefficients[step_index]
        lagrange = jnp.zeros_like(source)
        for sweep_index in range(ITERS):
            coupling = neighbour_sum(lagrange, ahead_list, behind_list, fault_coef[step_index], own_cells, other_cells)
            residual = jnp.concatenate([(source[0] + coupling)[None], source[1:]], axis=0)
            lagrange = apply_inverse(diag_inverse[step_index], residual)
        return lagrange
    late = solve(1, sources[1])
    early_source = sources[0] + jnp.stack([jnp.zeros_like(porosity), porosity * (late[0] - late[2]), porosity * (late[1] - late[2])])
    early = solve(0, early_source)
    solved = [early, late]
    flux_list = []
    porosity_terms = []
    for step_index in (1, 0):
        lagrange = solved[step_index]
        ahead_list, behind_list = coefficients[step_index]
        pressure_here = pressure[step_index]
        flux_grad = jnp.zeros_like(pressure_here)
        for direction in range(3):
            local_ahead = lax.optimization_barrier(jnp.sum(ahead_list[direction] * lagrange, axis=0))
            local_behind = lax.optimization_barrier(jnp.sum(behind_list[direction] * lagrange, axis=0))
            upper_term = lax.optimization_barrier(jnp.sum(ahead_list[direction] * shift_ahead(lagrange, direction + 1), axis=0))
            lower_term = lax.optimization_barrier(jnp.sum(behind_list[direction] * shift_behind(lagrange, direction + 1), axis=0))
            flux_grad = flux_grad + 0.5 * (pressure_here - shift_ahead(pressure_here, direction)) * (local_ahead - upper_term) + 0.5 * (shift_behind(pressure_here, direction) - pressure_here) * (lower_term - local_behind)
        flux_list.append(flux_grad)
        water_change = saturation[step_index + 1, 0] - saturation[step_index, 0]
        oil_change = saturation[step_index + 1, 1] - saturation[step_index, 1]
        porosity_terms.append(lagrange[0] * water_change + lagrange[1] * oil_change - lagrange[2] * (water_change + oil_change))
    log_perm_grad = explicit - (flux_list[0] + flux_list[1])
    porosity_gradient = -(porosity_terms[0] + porosity_terms[1])
    box_totals = jnp.stack([box_sums(log_perm_grad), box_sums(porosity_gradient)], axis=1)
    region_grad = jax.ops.segment_sum(box_totals, region_map.reshape(-1), num_segments=NREG).T
    return (jnp.stack([early, late]), region_grad)
```

```python
import functools

import jax
import jax.numpy as jnp
from jax import lax
from jax.experimental import pallas as pl
from jax.experimental.pallas import tpu as pltpu
from jax.sharding import PartitionSpec as P

ITERS = 6
BOX = 4
PARAM_REGIONS = 32
MESH = pl.DeviceIdType.MESH
HIGHEST = lax.Precision.HIGHEST

fluid_viscosity = (0.4, 0.5, 1.0)
sigma_sq = 64.0


def phase_mobility(water_sat, oil_sat):
    gas_sat = 1.0 - water_sat - oil_sat
    return [
        water_sat * water_sat / fluid_viscosity[0],
        oil_sat * oil_sat / fluid_viscosity[1],
        gas_sat * gas_sat / fluid_viscosity[2],
    ]


def mobility_slopes(water_sat, oil_sat):
    gas_sat = 1.0 - water_sat - oil_sat
    return (
        2.0 * water_sat / fluid_viscosity[0] - 2.0 * gas_sat / fluid_viscosity[2],
        2.0 * oil_sat / fluid_viscosity[1] - 2.0 * gas_sat / fluid_viscosity[2],
    )


def split_bf16(value):
    high = value.astype(jnp.bfloat16)
    return high, (value - high.astype(jnp.float32)).astype(jnp.bfloat16)


def kernel(
    counts,
    pressure_ref,
    saturation_ref,
    perm_ref,
    porosity_ref,
    flags_ref,
    inverse_ref,
    seismic_ref,
    well_rows_ref,
    well_cols_ref,
    well_top_ref,
    well_len_ref,
    bhp_ref,
    obs_ref,
    fault_row_ref,
    fault_z_ref,
    fault_trans_ref,
    fault_up_ref,
    fault_live_ref,
    lam_ref,
    box_ref,
    wp,
    wm,
    src,
    explicit,
    row_hot,
    z_hot,
    fault_coef,
    bx_s,
    by_s,
    bz_s,
    bx_r,
    by_r,
    bz_r,
    b_ss,
    b_rs,
    m_s,
    m_r,
    m_ss,
    m_rs,
    w_s,
    w_r,
    w_ss,
    w_rs,
    x_s,
    y_s,
    z_s,
    x_r,
    y_r,
    z_r,
    f_ss,
    f_rs,
    c_s,
    c_r,
    c_ss,
    c_rs,
):
    n_gx, n_gy, n_gz = counts
    here = (lax.axis_index("gx"), lax.axis_index("gy"), lax.axis_index("gz"))
    peers = n_gy * n_gz
    me = here[1] * n_gz + here[2]
    shape = perm_ref.shape
    nx, ny, nz = shape
    rows = nx * ny
    slots = m_r.shape[2]
    wide = peers * slots

    def toward(dim, step):
        moved = list(here)
        moved[dim] = lax.rem(here[dim] + step + counts[dim], counts[dim])
        return tuple(moved)

    def peer(offset):
        other = lax.rem(me + offset, peers)
        return (here[0], other // n_gz, lax.rem(other, n_gz))

    def remote(source, target, send, recv, device):
        return pltpu.make_async_remote_copy(
            src_ref=source,
            dst_ref=target,
            send_sem=send,
            recv_sem=recv,
            device_id=device,
            device_id_type=MESH,
        )

    m_r[...] = jnp.zeros_like(m_r)
    c_r[...] = jnp.zeros_like(c_r)

    barrier = pltpu.get_barrier_semaphore()
    for offset in range(1, peers):
        pl.semaphore_signal(barrier, inc=1, device_id=peer(offset), device_id_type=MESH)
    for step in (1, -1):
        pl.semaphore_signal(barrier, inc=1, device_id=toward(0, step), device_id_type=MESH)
    pl.semaphore_wait(barrier, peers + 1)

    xi = lax.broadcasted_iota(jnp.int32, shape, 0)
    yi = lax.broadcasted_iota(jnp.int32, shape, 1)
    zi = lax.broadcasted_iota(jnp.int32, shape, 2)
    iotas = (xi, yi, zi)
    diagonal = xi == zi

    def pack(column):
        return jnp.sum(jnp.where(diagonal, column, 0.0), axis=0)

    def unpack(tile):
        return jnp.sum(jnp.where(diagonal, tile[None], 0.0), axis=2, keepdims=True)

    def ahead(field, dim, halo):
        if dim == 0:
            return jnp.concatenate([field[1:], halo[None]], axis=0)
        last = shape[dim] - 1
        edge = halo if dim == 1 else unpack(halo)
        return jnp.where(iotas[dim] == last, edge, pltpu.roll(field, last, dim))

    def behind(field, dim, halo):
        if dim == 0:
            return jnp.concatenate([halo[None], field[:-1]], axis=0)
        edge = halo if dim == 1 else unpack(halo)
        return jnp.where(iotas[dim] == 0, edge, pltpu.roll(field, 1, dim))

    perm = perm_ref[...]
    flags = flags_ref[...].astype(jnp.float32)
    pressure = [pressure_ref[t] for t in range(2)]
    mobility = [
        phase_mobility(saturation_ref[t + 1, 0], saturation_ref[t + 1, 1]) for t in range(2)
    ]
    bundle = [perm] + mobility[0] + mobility[1] + [flags] + pressure
    for q, field in enumerate(bundle):
        bx_s[0, q] = field[nx - 1]
        bx_s[1, q] = field[0]
        by_s[0, q] = field[:, ny - 1 :, :]
        by_s[1, q] = field[:, :1, :]
        bz_s[0, q] = pack(field[:, :, nz - 1 :])
        bz_s[1, q] = pack(field[:, :, :1])
    b_copies = []
    for dim, (sent, got) in enumerate(((bx_s, bx_r), (by_s, by_r), (bz_s, bz_r))):
        for side, step in ((0, 1), (1, -1)):
            copy = remote(
                sent.at[side],
                got.at[side],
                b_ss.at[dim, side],
                b_rs.at[dim, side],
                toward(dim, step),
            )
            copy.start()
            b_copies.append(copy)

    fault_z = fault_z_ref[...]
    hot = (lax.broadcasted_iota(jnp.int32, (rows, wide), 0) == fault_row_ref[...]).astype(
        jnp.float32
    ).astype(jnp.bfloat16)
    row_hot[:rows] = hot
    row_hot[rows:] = hot
    z_hot[...] = (
        (lax.broadcasted_iota(jnp.int32, (nz, wide), 0) == fault_z)
        .astype(jnp.float32)
        .astype(jnp.bfloat16)
    )

    def gather(fields):
        stacked = []
        for field in fields:
            stacked.append(
                jnp.concatenate(split_bf16(field.reshape(rows, nz).T), axis=1)
            )
        columns = jnp.dot(
            jnp.concatenate(stacked, axis=0), row_hot[...], preferred_element_type=jnp.float32
        )
        chosen = lax.broadcasted_iota(jnp.int32, (nz, wide), 0) == fault_z
        return [
            jnp.sum(
                jnp.where(chosen, columns[k * nz : (k + 1) * nz], 0.0), axis=0, keepdims=True
            )
            for k in range(len(fields))
        ]

    own = gather(mobility[0]) + gather(mobility[1])
    for p in range(peers):
        for q in range(6):
            m_s[p, q : q + 1, :] = own[q][:, p * slots : (p + 1) * slots]
        m_s[p, 6:8, :] = jnp.zeros((2, slots), jnp.float32)
    m_copies = []
    for offset in range(1, peers):
        other = lax.rem(me + offset, peers)
        copy = remote(
            m_s.at[other], m_r.at[me], m_ss.at[offset], m_rs.at[offset], peer(offset)
        )
        copy.start()
        m_copies.append(copy)

    n_wells = well_top_ref.shape[0]
    well_hot = (
        lax.broadcasted_iota(jnp.int32, (n_wells, rows), 1) == well_rows_ref[...]
    ).astype(jnp.float32)
    well_hot_t = (
        lax.broadcasted_iota(jnp.int32, (rows, n_wells), 0) == well_cols_ref[...]
    ).astype(jnp.float32)
    depth = here[2] * nz + lax.broadcasted_iota(jnp.int32, (n_wells, nz), 1)
    top = well_top_ref[...]
    perforated = ((depth >= top) & (depth < top + well_len_ref[...])).astype(jnp.float32)
    total = [perm * (mobility[t][0] + mobility[t][1] + mobility[t][2]) for t in range(2)]
    lane = lax.broadcasted_iota(jnp.int32, (n_wells, nz), 1)
    rates = jnp.zeros((n_wells, nz), jnp.float32)
    for t in range(2):
        with_pressure = jnp.dot(
            well_hot,
            (total[t] * pressure[t]).reshape(rows, nz),
            precision=HIGHEST,
            preferred_element_type=jnp.float32,
        )
        without = jnp.dot(
            well_hot,
            total[t].reshape(rows, nz),
            precision=HIGHEST,
            preferred_element_type=jnp.float32,
        )
        rate = jnp.sum(
            perforated * (with_pressure - bhp_ref[t] * without), axis=1, keepdims=True
        )
        rates = jnp.where(lane == t, rate, rates)
    w_s[...] = rates
    w_copies = []
    for offset in range(1, n_gz):
        copy = remote(
            w_s, w_r.at[offset], w_ss.at[offset], w_rs.at[offset], toward(2, offset)
        )
        copy.start()
        w_copies.append(copy)

    for copy in b_copies:
        copy.wait()
    halos = ((bx_r, bx_s), (by_r, by_s), (bz_r, bz_s))
    for dim in range(3):
        got = halos[dim][0]
        up_ok = (here[dim] < counts[dim] - 1).astype(jnp.float32)
        low_ok = (here[dim] > 0).astype(jnp.float32)
        up_face = jnp.sqrt(perm * ahead(perm, dim, got[1, 0]))
        up_face = up_face * jnp.where(iotas[dim] == shape[dim] - 1, up_ok, 1.0)
        low_face = jnp.sqrt(perm * behind(perm, dim, got[0, 0]))
        low_face = low_face * jnp.where(iotas[dim] == 0, low_ok, 1.0)
        own_flags = flags.astype(jnp.int32)
        low_flags = behind(flags, dim, got[0, 7]).astype(jnp.int32)
        for t in range(2):
            bit = 3 * t + dim
            own_up = jnp.bitwise_and(jnp.right_shift(own_flags, bit), 1) == 1
            low_up = jnp.bitwise_and(jnp.right_shift(low_flags, bit), 1) == 1
            for k in range(3):
                q = 1 + 3 * t + k
                m = mobility[t][k]
                wp[t, dim, k] = up_face * jnp.where(own_up, m, ahead(m, dim, got[1, q]))
                wm[t, dim, k] = low_face * jnp.where(low_up, behind(m, dim, got[0, q]), m)

    for copy in m_copies:
        copy.wait()
    for t in range(2):
        own_up = jnp.bitwise_and(jnp.right_shift(fault_up_ref[...], t), 1) == 1
        scale = fault_trans_ref[...] * fault_live_ref[...]
        for k in range(3):
            q = 3 * t + k
            other = jnp.concatenate([m_r[p, q : q + 1, :] for p in range(peers)], axis=1)
            fault_coef[q : q + 1, :] = scale * jnp.where(own_up, own[q], other)

    for copy in w_copies:
        copy.wait()
    rates = w_s[...]
    for offset in range(1, n_gz):
        rates = rates + w_r[offset]
    explicit_sum = jnp.zeros(shape, jnp.float32)
    for t in range(2):
        misfit = (rates[:, t : t + 1] - obs_ref[t]) / sigma_sq
        weight = misfit * perforated
        spread = jnp.dot(
            well_hot_t, weight, precision=HIGHEST, preferred_element_type=jnp.float32
        ).reshape(shape)
        spread_bhp = jnp.dot(
            well_hot_t, weight * bhp_ref[t], precision=HIGHEST, preferred_element_type=jnp.float32
        ).reshape(shape)
        drawn = pressure[t] * spread - spread_bhp
        water_slope, oil_slope = mobility_slopes(
            saturation_ref[t + 1, 0], saturation_ref[t + 1, 1]
        )
        src[t, 0] = total[t] * spread
        water_source = perm * drawn * water_slope
        if t == 1:
            water_source = water_source + saturation_ref[2, 0] - seismic_ref[...]
        src[t, 1] = water_source
        src[t, 2] = perm * drawn * oil_slope
        explicit_sum = explicit_sum + total[t] * drawn
    explicit[...] = explicit_sum

    def relax(t, coupling):
        residual = [src[t, u] for u in range(3)]
        if coupling is not None:
            residual[0] = residual[0] + coupling
        for k in range(3):
            lam_ref[t, k] = (
                inverse_ref[t, 0, k] * residual[0]
                + inverse_ref[t, 1, k] * residual[1]
                + inverse_ref[t, 2, k] * residual[2]
            )

    def face_copies(slot):
        made = []
        for dim, (sent, got) in enumerate(((x_s, x_r), (y_s, y_r), (z_s, z_r))):
            for side, step in ((0, 1), (1, -1)):
                made.append(
                    remote(
                        sent.at[side],
                        got.at[slot, side],
                        f_ss.at[dim, side],
                        f_rs.at[slot, dim, side],
                        toward(dim, step),
                    )
                )
        return made

    def products(t):
        lam = [lam_ref[t, k] for k in range(3)]
        up = []
        down = []
        for dim in range(3):
            up.append(sum(wp[t, dim, k] * lam[k] for k in range(3)))
            down.append(sum(wm[t, dim, k] * lam[k] for k in range(3)))
        x_s[0] = up[0][nx - 1]
        x_s[1] = down[0][0]
        y_s[0] = up[1][:, ny - 1 :, :]
        y_s[1] = down[1][:, :1, :]
        z_s[0] = pack(up[2][:, :, nz - 1 :])
        z_s[1] = pack(down[2][:, :, :1])
        return lam, up, down

    def terms(up, down, slot):
        faces = (x_r, y_r, z_r)
        upper = [ahead(down[dim], dim, faces[dim][slot, 1]) for dim in range(3)]
        lower = [behind(up[dim], dim, faces[dim][slot, 0]) for dim in range(3)]
        return upper, lower

    def sweep(t, n_face, n_fault):
        face_slot = lax.rem(n_face, 2)
        slot = lax.rem(n_fault, 2)
        lam, up, down = products(t)
        faces = face_copies(face_slot)
        for copy in faces:
            copy.start()
        values = gather(lam)
        sent = sum(
            fault_coef[3 * t + k : 3 * t + k + 1, :] * values[k] for k in range(3)
        )
        for p in range(peers):
            c_s[p] = sent[:, p * slots : (p + 1) * slots]
        copies = []
        for offset in range(1, peers):
            other = lax.rem(me + offset, peers)
            copy = remote(
                c_s.at[other],
                c_r.at[slot, me],
                c_ss.at[offset],
                c_rs.at[slot, offset],
                peer(offset),
            )
            copy.start()
            copies.append(copy)
        for copy in faces:
            copy.wait()
        upper, lower = terms(up, down, face_slot)
        coupling = upper[0] + lower[0] + upper[1] + lower[1] + upper[2] + lower[2]
        for copy in copies:
            copy.wait()
        arrived = jnp.concatenate([c_r[slot, p] for p in range(peers)], axis=1)
        picked = jnp.where(
            lax.broadcasted_iota(jnp.int32, (rows, wide), 0) == fault_row_ref[...], arrived, 0.0
        )
        both = jnp.concatenate(split_bf16(picked), axis=0)
        added = lax.dot_general(
            both,
            z_hot[...],
            (((1,), (1,)), ((), ())),
            preferred_element_type=jnp.float32,
        )
        coupling = coupling + (added[:rows] + added[rows:]).reshape(shape)
        relax(t, coupling)

    log_perm = explicit_sum
    for turn, t in enumerate((1, 0)):
        if t == 0:
            porosity = porosity_ref[...]
            src[0, 1] += porosity * (lam_ref[1, 0] - lam_ref[1, 2])
            src[0, 2] += porosity * (lam_ref[1, 1] - lam_ref[1, 2])
        relax(t, None)

        def body(step, carry, t=t, turn=turn):
            sweep(t, turn * ITERS + step, turn * (ITERS - 1) + step)
            return carry

        lax.fori_loop(0, ITERS - 1, body, 0)
        slot = (turn * ITERS + ITERS - 1) % 2
        lam, up, down = products(t)
        faces = face_copies(slot)
        for copy in faces:
            copy.start()
        for copy in faces:
            copy.wait()
        upper, lower = terms(up, down, slot)
        p_here = pressure_ref[t]
        flux = jnp.zeros(shape, jnp.float32)
        for dim in range(3):
            got = halos[dim][0]
            flux = (
                flux
                + 0.5
                * (p_here - ahead(p_here, dim, got[1, 8 + t]))
                * (up[dim] - upper[dim])
                + 0.5
                * (behind(p_here, dim, got[0, 8 + t]) - p_here)
                * (lower[dim] - down[dim])
            )
        explicit[...] -= flux

    porosity_sum = jnp.zeros(shape, jnp.float32)
    for t in range(2):
        water = saturation_ref[t + 1, 0] - saturation_ref[t, 0]
        oil = saturation_ref[t + 1, 1] - saturation_ref[t, 1]
        porosity_sum = porosity_sum + (
            lam_ref[t, 0] * water + lam_ref[t, 1] * oil - lam_ref[t, 2] * (water + oil)
        )
    z_boxes = (
        lax.broadcasted_iota(jnp.int32, (nz, nz), 0) // BOX
        == lax.broadcasted_iota(jnp.int32, (nz, nz), 1)
    ).astype(jnp.float32)
    for q, field in enumerate((explicit[...], -porosity_sum)):
        in_x = jnp.sum(field.reshape(nx // BOX, BOX, ny, nz), axis=1)
        box_ref[q] = jnp.dot(
            in_x.reshape(nx // BOX * ny, nz),
            z_boxes,
            precision=HIGHEST,
            preferred_element_type=jnp.float32,
        )


def local(
    pressure,
    saturation,
    permeability,
    porosity,
    upwind_flags,
    diag_inverse,
    seismic_obs,
    well_x,
    well_y,
    well_top,
    well_len,
    well_bhp,
    well_obs,
    fault_cell,
    fault_count,
    fault_trans,
    fault_up,
    region_map,
):
    counts = tuple(lax.axis_size(axis) for axis in ("gx", "gy", "gz"))
    nx, ny, nz = permeability.shape
    peers, slots = fault_cell.shape[1:]
    wide = peers * slots
    n_wells = well_x.shape[2]
    well_row = well_x[0, 0] * ny + well_y[0, 0]
    cells = fault_cell[0]
    live = (
        jnp.arange(slots, dtype=jnp.int32)[None, :] < fault_count[0][:, None]
    ).astype(jnp.float32)
    vmem = pl.BlockSpec(memory_space=pltpu.VMEM)
    f32 = jnp.float32
    dma = pltpu.SemaphoreType.DMA
    faces = [(2, ny, nz), (2, nx, 1, nz), (2, ny, nz)]
    bundles = [(2, 10, ny, nz), (2, 10, nx, 1, nz), (2, 10, ny, nz)]
    scratch = [
        pltpu.VMEM((2, 3, 3, nx, ny, nz), f32),
        pltpu.VMEM((2, 3, 3, nx, ny, nz), f32),
        pltpu.VMEM((2, 3, nx, ny, nz), f32),
        pltpu.VMEM((nx, ny, nz), f32),
        pltpu.VMEM((2 * nx * ny, wide), jnp.bfloat16),
        pltpu.VMEM((nz, wide), jnp.bfloat16),
        pltpu.VMEM((8, wide), f32),
        *[pltpu.VMEM(s, f32) for s in bundles],
        *[pltpu.VMEM(s, f32) for s in bundles],
        dma((3, 2)),
        dma((3, 2)),
        pltpu.VMEM((peers, 8, slots), f32),
        pltpu.VMEM((peers, 8, slots), f32),
        dma((peers,)),
        dma((peers,)),
        pltpu.VMEM((n_wells, nz), f32),
        pltpu.VMEM((counts[2], n_wells, nz), f32),
        dma((counts[2],)),
        dma((counts[2],)),
        *[pltpu.VMEM(s, f32) for s in faces],
        *[pltpu.VMEM((2,) + s, f32) for s in faces],
        dma((3, 2)),
        dma((2, 3, 2)),
        pltpu.VMEM((peers, 1, slots), f32),
        pltpu.VMEM((2, peers, 1, slots), f32),
        dma((peers,)),
        dma((2, peers)),
    ]
    adjoint, boxes = pl.pallas_call(
        functools.partial(kernel, counts),
        out_shape=(
            jax.ShapeDtypeStruct((2, 3, nx, ny, nz), f32),
            jax.ShapeDtypeStruct((2, nx // BOX * ny, nz), f32),
        ),
        in_specs=[vmem] * 18,
        out_specs=(vmem, vmem),
        scratch_shapes=scratch,
        compiler_params=pltpu.CompilerParams(
            collective_id=0, has_side_effects=True, vmem_limit_bytes=48 * 2**20
        ),
    )(
        pressure,
        saturation,
        permeability,
        porosity,
        upwind_flags,
        diag_inverse,
        seismic_obs,
        well_row[:, None],
        well_row[None, :],
        well_top[0, 0][:, None],
        well_len[0, 0][:, None],
        well_bhp[:, 0, 0][:, :, None],
        well_obs[:, 0, 0][:, :, None],
        (cells // nz).reshape(1, wide),
        (cells % nz).reshape(1, wide),
        fault_trans[0].reshape(1, wide),
        fault_up[0].reshape(1, wide),
        live.reshape(1, wide),
    )
    box_totals = boxes[:, :, : nz // BOX].reshape(2, nx // BOX, ny // BOX, BOX, nz // BOX)
    box_totals = jnp.sum(box_totals, axis=3).reshape(2, -1)
    region_labels = PARAM_REGIONS * counts[0] * counts[1] * counts[2]
    chosen = (
        region_map.reshape(-1)[:, None] == jnp.arange(region_labels, dtype=jnp.int32)[None, :]
    ).astype(f32)
    region_partial = jnp.dot(box_totals, chosen, precision=HIGHEST)
    region_grad = lax.psum_scatter(
        region_partial, ("gx", "gy", "gz"), scatter_dimension=1, tiled=True
    )
    return (adjoint, region_grad)


def solution(mesh):
    placed = (
        P(None, "gx", "gy", "gz"),
        P(None, None, "gx", "gy", "gz"),
        P("gx", "gy", "gz"),
        P("gx", "gy", "gz"),
        P("gx", "gy", "gz"),
        P(None, None, None, "gx", "gy", "gz"),
        P("gx", "gy", "gz"),
        P("gx", "gy", None),
        P("gx", "gy", None),
        P("gx", "gy", None),
        P("gx", "gy", None),
        P(None, "gx", "gy", None),
        P(None, "gx", "gy", None),
        P(("gx", "gy", "gz"), None, None),
        P(("gx", "gy", "gz"), None),
        P(("gx", "gy", "gz"), None, None),
        P(("gx", "gy", "gz"), None, None),
        P("gx", "gy", "gz"),
    )
    return jax.shard_map(
        local,
        mesh=mesh,
        in_specs=placed,
        out_specs=(P(None, None, "gx", "gy", "gz"), P(None, ("gx", "gy", "gz"))),
        check_vma=False,
    )
```

```python
import functools

import jax
import jax.numpy as jnp
from jax import lax
from jax.experimental import pallas as pl
from jax.experimental.pallas import tpu as pltpu
from jax.sharding import PartitionSpec as P

ITERS = 6
BOX = 4
PARAM_REGIONS = 32
MESH = pl.DeviceIdType.MESH
HIGHEST = lax.Precision.HIGHEST

fluid_viscosity = (0.4, 0.5, 1.0)
sigma_sq = 64.0


def phase_mobility(water_sat, oil_sat):
    gas_sat = 1.0 - water_sat - oil_sat
    return [
        water_sat * water_sat / fluid_viscosity[0],
        oil_sat * oil_sat / fluid_viscosity[1],
        gas_sat * gas_sat / fluid_viscosity[2],
    ]


def mobility_slopes(water_sat, oil_sat):
    gas_sat = 1.0 - water_sat - oil_sat
    return (
        2.0 * water_sat / fluid_viscosity[0] - 2.0 * gas_sat / fluid_viscosity[2],
        2.0 * oil_sat / fluid_viscosity[1] - 2.0 * gas_sat / fluid_viscosity[2],
    )


def split_bf16(value):
    high = value.astype(jnp.bfloat16)
    return high, (value - high.astype(jnp.float32)).astype(jnp.bfloat16)


def kernel(
    counts,
    pressure_hbm,
    saturation_hbm,
    perm_hbm,
    porosity_hbm,
    flags_hbm,
    inverse_hbm,
    seismic_hbm,
    well_x_ref,
    well_y_ref,
    well_top_ref,
    well_len_ref,
    bhp_ref,
    obs_ref,
    fault_cell_ref,
    fault_count_ref,
    fault_trans_ref,
    fault_up_ref,
    map_ref,
    lam_ref,
    region_ref,
    pressure_ref,
    saturation_ref,
    perm_ref,
    porosity_ref,
    flags_ref,
    inverse_ref,
    seismic_ref,
    in_sem,
    wp,
    wm,
    src,
    explicit,
    row_hot,
    z_hot,
    fault_coef,
    bx_s,
    by_s,
    bz_s,
    bx_r,
    by_r,
    bz_r,
    b_ss,
    b_rs,
    m_s,
    m_r,
    m_ss,
    m_rs,
    w_s,
    w_r,
    w_ss,
    w_rs,
    x_s,
    y_s,
    z_s,
    x_r,
    y_r,
    z_r,
    f_ss,
    f_rs,
    c_s,
    c_r,
    c_ss,
    c_rs,
    g_s,
    g_r,
    g_ss,
    g_rs,
    r_s,
    r_r,
    r_ss,
    r_rs,
):
    n_gx, n_gy, n_gz = counts
    here = (lax.axis_index("gx"), lax.axis_index("gy"), lax.axis_index("gz"))
    peers = n_gy * n_gz
    me = here[1] * n_gz + here[2]
    shape = perm_ref.shape
    nx, ny, nz = shape
    rows = nx * ny
    slots = m_r.shape[2]
    wide = peers * slots

    def toward(dim, step):
        moved = list(here)
        moved[dim] = lax.rem(here[dim] + step + counts[dim], counts[dim])
        return tuple(moved)

    def peer(offset):
        other = lax.rem(me + offset, peers)
        return (here[0], other // n_gz, lax.rem(other, n_gz))

    def remote(source, target, send, recv, device):
        return pltpu.make_async_remote_copy(
            src_ref=source,
            dst_ref=target,
            send_sem=send,
            recv_sem=recv,
            device_id=device,
            device_id_type=MESH,
        )

    loads = [
        pltpu.make_async_copy(source, target, in_sem.at[n])
        for n, (source, target) in enumerate(
            (
                (perm_hbm, perm_ref),
                (saturation_hbm, saturation_ref),
                (flags_hbm, flags_ref),
                (pressure_hbm, pressure_ref),
                (seismic_hbm, seismic_ref),
                (inverse_hbm, inverse_ref),
                (porosity_hbm, porosity_ref),
            )
        )
    ]
    for load in loads:
        load.start()
    m_r[...] = jnp.zeros_like(m_r)
    c_r[...] = jnp.zeros_like(c_r)

    barrier = pltpu.get_barrier_semaphore()
    for offset in range(1, peers):
        pl.semaphore_signal(barrier, inc=1, device_id=peer(offset), device_id_type=MESH)
    for step in range(1, n_gx):
        pl.semaphore_signal(barrier, inc=1, device_id=toward(0, step), device_id_type=MESH)
    pl.semaphore_wait(barrier, peers - 1 + n_gx - 1)
    for load in loads[:4]:
        load.wait()

    xi = lax.broadcasted_iota(jnp.int32, shape, 0)
    yi = lax.broadcasted_iota(jnp.int32, shape, 1)
    zi = lax.broadcasted_iota(jnp.int32, shape, 2)
    iotas = (xi, yi, zi)
    diagonal = xi == zi

    def pack(column):
        return jnp.sum(jnp.where(diagonal, column, 0.0), axis=0)

    def unpack(tile):
        return jnp.sum(jnp.where(diagonal, tile[None], 0.0), axis=2, keepdims=True)

    def ahead(field, dim, halo):
        if dim == 0:
            return jnp.concatenate([field[1:], halo[None]], axis=0)
        last = shape[dim] - 1
        edge = halo if dim == 1 else unpack(halo)
        return jnp.where(iotas[dim] == last, edge, pltpu.roll(field, last, dim))

    def behind(field, dim, halo):
        if dim == 0:
            return jnp.concatenate([halo[None], field[:-1]], axis=0)
        edge = halo if dim == 1 else unpack(halo)
        return jnp.where(iotas[dim] == 0, edge, pltpu.roll(field, 1, dim))

    perm = perm_ref[...]
    flags = flags_ref[...].astype(jnp.float32)
    pressure = [pressure_ref[t] for t in range(2)]
    mobility = [
        phase_mobility(saturation_ref[t + 1, 0], saturation_ref[t + 1, 1]) for t in range(2)
    ]
    bundle = [perm] + mobility[0] + mobility[1] + [flags] + pressure
    for q, field in enumerate(bundle):
        bx_s[0, q] = field[nx - 1]
        bx_s[1, q] = field[0]
        by_s[0, q] = field[:, ny - 1 :, :]
        by_s[1, q] = field[:, :1, :]
        bz_s[0, q] = pack(field[:, :, nz - 1 :])
        bz_s[1, q] = pack(field[:, :, :1])
    b_copies = []
    for dim, (sent, got) in enumerate(((bx_s, bx_r), (by_s, by_r), (bz_s, bz_r))):
        for side, step in ((0, 1), (1, -1)):
            copy = remote(
                sent.at[side],
                got.at[side],
                b_ss.at[dim, side],
                b_rs.at[dim, side],
                toward(dim, step),
            )
            copy.start()
            b_copies.append(copy)

    def as_row(ref):
        return jnp.concatenate([ref[0, p : p + 1, :] for p in range(peers)], axis=1)

    fault_cell = as_row(fault_cell_ref)
    fault_row = fault_cell // nz
    fault_z = fault_cell - fault_row * nz
    hot = (lax.broadcasted_iota(jnp.int32, (rows, wide), 0) == fault_row).astype(
        jnp.float32
    ).astype(jnp.bfloat16)
    row_hot[:rows] = hot
    row_hot[rows:] = hot
    z_hot[...] = (
        (lax.broadcasted_iota(jnp.int32, (nz, wide), 0) == fault_z)
        .astype(jnp.float32)
        .astype(jnp.bfloat16)
    )

    def gather(fields):
        stacked = []
        for field in fields:
            stacked.append(
                jnp.concatenate(split_bf16(field.reshape(rows, nz).T), axis=1)
            )
        columns = jnp.dot(
            jnp.concatenate(stacked, axis=0), row_hot[...], preferred_element_type=jnp.float32
        )
        chosen = lax.broadcasted_iota(jnp.int32, (nz, wide), 0) == fault_z
        return [
            jnp.sum(
                jnp.where(chosen, columns[k * nz : (k + 1) * nz], 0.0), axis=0, keepdims=True
            )
            for k in range(len(fields))
        ]

    own = gather(mobility[0]) + gather(mobility[1])
    for p in range(peers):
        for q in range(6):
            m_s[p, q : q + 1, :] = own[q][:, p * slots : (p + 1) * slots]
        m_s[p, 6:8, :] = jnp.zeros((2, slots), jnp.float32)
    m_copies = []
    for offset in range(1, peers):
        other = lax.rem(me + offset, peers)
        copy = remote(
            m_s.at[other], m_r.at[me], m_ss.at[offset], m_rs.at[offset], peer(offset)
        )
        copy.start()
        m_copies.append(copy)

    n_wells = well_top_ref.shape[2]
    eye = lax.broadcasted_iota(jnp.int32, (n_wells, n_wells), 0) == lax.broadcasted_iota(
        jnp.int32, (n_wells, n_wells), 1
    )

    def as_column(row):
        return jnp.sum(jnp.where(eye, row.astype(jnp.float32), 0.0), axis=1, keepdims=True)

    well_row = well_x_ref[0] * ny + well_y_ref[0]
    bhp = [as_column(bhp_ref[t, 0]) for t in range(2)]
    well_hot = (
        lax.broadcasted_iota(jnp.int32, (n_wells, rows), 1).astype(jnp.float32)
        == as_column(well_row)
    ).astype(jnp.float32)
    well_hot_t = (
        lax.broadcasted_iota(jnp.int32, (rows, n_wells), 0) == well_row
    ).astype(jnp.float32)
    depth = (here[2] * nz + lax.broadcasted_iota(jnp.int32, (n_wells, nz), 1)).astype(
        jnp.float32
    )
    top = as_column(well_top_ref[0])
    bottom = as_column(well_top_ref[0] + well_len_ref[0])
    perforated = jnp.where((depth >= top) & (depth < bottom), 1.0, 0.0)
    total = [perm * (mobility[t][0] + mobility[t][1] + mobility[t][2]) for t in range(2)]
    lane = lax.broadcasted_iota(jnp.int32, (n_wells, nz), 1)
    rates = jnp.zeros((n_wells, nz), jnp.float32)
    for t in range(2):
        with_pressure = jnp.dot(
            well_hot,
            (total[t] * pressure[t]).reshape(rows, nz),
            precision=HIGHEST,
            preferred_element_type=jnp.float32,
        )
        without = jnp.dot(
            well_hot,
            total[t].reshape(rows, nz),
            precision=HIGHEST,
            preferred_element_type=jnp.float32,
        )
        rate = jnp.sum(
            perforated * (with_pressure - bhp[t] * without), axis=1, keepdims=True
        )
        rates = jnp.where(lane == t, rate, rates)
    w_s[...] = rates
    w_copies = []
    for offset in range(1, n_gz):
        copy = remote(
            w_s, w_r.at[offset], w_ss.at[offset], w_rs.at[offset], toward(2, offset)
        )
        copy.start()
        w_copies.append(copy)

    for copy in b_copies:
        copy.wait()
    halos = ((bx_r, bx_s), (by_r, by_s), (bz_r, bz_s))
    for dim in range(3):
        got = halos[dim][0]
        up_ok = (here[dim] < counts[dim] - 1).astype(jnp.float32)
        low_ok = (here[dim] > 0).astype(jnp.float32)
        up_face = jnp.sqrt(perm * ahead(perm, dim, got[1, 0]))
        up_face = up_face * jnp.where(iotas[dim] == shape[dim] - 1, up_ok, 1.0)
        low_face = jnp.sqrt(perm * behind(perm, dim, got[0, 0]))
        low_face = low_face * jnp.where(iotas[dim] == 0, low_ok, 1.0)
        own_flags = flags.astype(jnp.int32)
        low_flags = behind(flags, dim, got[0, 7]).astype(jnp.int32)
        for t in range(2):
            bit = 3 * t + dim
            own_up = jnp.bitwise_and(jnp.right_shift(own_flags, bit), 1) == 1
            low_up = jnp.bitwise_and(jnp.right_shift(low_flags, bit), 1) == 1
            for k in range(3):
                q = 1 + 3 * t + k
                m = mobility[t][k]
                wp[t, dim, k] = up_face * jnp.where(own_up, m, ahead(m, dim, got[1, q]))
                wm[t, dim, k] = low_face * jnp.where(low_up, behind(m, dim, got[0, q]), m)

    for copy in m_copies:
        copy.wait()
    slot_index = lax.broadcasted_iota(jnp.int32, (1, slots), 1)
    scale = jnp.concatenate(
        [
            jnp.where(
                slot_index < fault_count_ref[:, p : p + 1], fault_trans_ref[0, p : p + 1, :], 0.0
            )
            for p in range(peers)
        ],
        axis=1,
    )
    fault_up = as_row(fault_up_ref)
    for t in range(2):
        own_up = jnp.bitwise_and(jnp.right_shift(fault_up, t), 1) == 1
        for k in range(3):
            q = 3 * t + k
            other = jnp.concatenate([m_r[p, q : q + 1, :] for p in range(peers)], axis=1)
            fault_coef[q : q + 1, :] = scale * jnp.where(own_up, own[q], other)

    for copy in w_copies:
        copy.wait()
    for load in loads[4:]:
        load.wait()
    rates = w_s[...]
    for offset in range(1, n_gz):
        rates = rates + w_r[offset]
    explicit_sum = jnp.zeros(shape, jnp.float32)
    for t in range(2):
        misfit = (rates[:, t : t + 1] - as_column(obs_ref[t, 0])) / sigma_sq
        weight = misfit * perforated
        spread = jnp.dot(
            well_hot_t, weight, precision=HIGHEST, preferred_element_type=jnp.float32
        ).reshape(shape)
        spread_bhp = jnp.dot(
            well_hot_t, weight * bhp[t], precision=HIGHEST, preferred_element_type=jnp.float32
        ).reshape(shape)
        drawn = pressure[t] * spread - spread_bhp
        water_slope, oil_slope = mobility_slopes(
            saturation_ref[t + 1, 0], saturation_ref[t + 1, 1]
        )
        src[t, 0] = total[t] * spread
        water_source = perm * drawn * water_slope
        if t == 1:
            water_source = water_source + saturation_ref[2, 0] - seismic_ref[...]
        src[t, 1] = water_source
        src[t, 2] = perm * drawn * oil_slope
        explicit_sum = explicit_sum + total[t] * drawn
    explicit[...] = explicit_sum

    def relax(t, coupling):
        residual = [src[t, u] for u in range(3)]
        if coupling is not None:
            residual[0] = residual[0] + coupling
        for k in range(3):
            lam_ref[t, k] = (
                inverse_ref[t, 0, k] * residual[0]
                + inverse_ref[t, 1, k] * residual[1]
                + inverse_ref[t, 2, k] * residual[2]
            )

    def face_copies(slot):
        made = []
        for dim, (sent, got) in enumerate(((x_s, x_r), (y_s, y_r), (z_s, z_r))):
            for side, step in ((0, 1), (1, -1)):
                made.append(
                    remote(
                        sent.at[side],
                        got.at[slot, side],
                        f_ss.at[dim, side],
                        f_rs.at[slot, dim, side],
                        toward(dim, step),
                    )
                )
        return made

    def products(t):
        lam = [lam_ref[t, k] for k in range(3)]
        up = []
        down = []
        for dim in range(3):
            up.append(sum(wp[t, dim, k] * lam[k] for k in range(3)))
            down.append(sum(wm[t, dim, k] * lam[k] for k in range(3)))
        x_s[0] = up[0][nx - 1]
        x_s[1] = down[0][0]
        y_s[0] = up[1][:, ny - 1 :, :]
        y_s[1] = down[1][:, :1, :]
        z_s[0] = pack(up[2][:, :, nz - 1 :])
        z_s[1] = pack(down[2][:, :, :1])
        return lam, up, down

    def terms(up, down, slot):
        faces = (x_r, y_r, z_r)
        upper = [ahead(down[dim], dim, faces[dim][slot, 1]) for dim in range(3)]
        lower = [behind(up[dim], dim, faces[dim][slot, 0]) for dim in range(3)]
        return upper, lower

    def sweep(t, n_face, n_fault):
        face_slot = lax.rem(n_face, 2)
        slot = lax.rem(n_fault, 2)
        lam, up, down = products(t)
        faces = face_copies(face_slot)
        for copy in faces:
            copy.start()
        values = gather(lam)
        sent = sum(
            fault_coef[3 * t + k : 3 * t + k + 1, :] * values[k] for k in range(3)
        )
        for p in range(peers):
            c_s[p] = sent[:, p * slots : (p + 1) * slots]
        copies = []
        for offset in range(1, peers):
            other = lax.rem(me + offset, peers)
            copy = remote(
                c_s.at[other],
                c_r.at[slot, me],
                c_ss.at[offset],
                c_rs.at[slot, offset],
                peer(offset),
            )
            copy.start()
            copies.append(copy)
        for copy in faces:
            copy.wait()
        upper, lower = terms(up, down, face_slot)
        coupling = upper[0] + lower[0] + upper[1] + lower[1] + upper[2] + lower[2]
        for copy in copies:
            copy.wait()
        arrived = jnp.concatenate([c_r[slot, p] for p in range(peers)], axis=1)
        picked = jnp.where(
            lax.broadcasted_iota(jnp.int32, (rows, wide), 0) == fault_row, arrived, 0.0
        )
        both = jnp.concatenate(split_bf16(picked), axis=0)
        added = lax.dot_general(
            both,
            z_hot[...],
            (((1,), (1,)), ((), ())),
            preferred_element_type=jnp.float32,
        )
        coupling = coupling + (added[:rows] + added[rows:]).reshape(shape)
        relax(t, coupling)

    log_perm = explicit_sum
    for turn, t in enumerate((1, 0)):
        if t == 0:
            porosity = porosity_ref[...]
            src[0, 1] += porosity * (lam_ref[1, 0] - lam_ref[1, 2])
            src[0, 2] += porosity * (lam_ref[1, 1] - lam_ref[1, 2])
        relax(t, None)

        def body(step, carry, t=t, turn=turn):
            sweep(t, turn * ITERS + step, turn * (ITERS - 1) + step)
            return carry

        lax.fori_loop(0, ITERS - 1, body, 0)
        slot = (turn * ITERS + ITERS - 1) % 2
        lam, up, down = products(t)
        faces = face_copies(slot)
        for copy in faces:
            copy.start()
        for copy in faces:
            copy.wait()
        upper, lower = terms(up, down, slot)
        p_here = pressure_ref[t]
        flux = jnp.zeros(shape, jnp.float32)
        for dim in range(3):
            got = halos[dim][0]
            flux = (
                flux
                + 0.5
                * (p_here - ahead(p_here, dim, got[1, 8 + t]))
                * (up[dim] - upper[dim])
                + 0.5
                * (behind(p_here, dim, got[0, 8 + t]) - p_here)
                * (lower[dim] - down[dim])
            )
        explicit[...] -= flux

    porosity_sum = jnp.zeros(shape, jnp.float32)
    for t in range(2):
        water = saturation_ref[t + 1, 0] - saturation_ref[t, 0]
        oil = saturation_ref[t + 1, 1] - saturation_ref[t, 1]
        porosity_sum = porosity_sum + (
            lam_ref[t, 0] * water + lam_ref[t, 1] * oil - lam_ref[t, 2] * (water + oil)
        )
    z_boxes = (
        lax.broadcasted_iota(jnp.int32, (nz, nz), 0) // BOX
        == lax.broadcasted_iota(jnp.int32, (nz, nz), 1)
    ).astype(jnp.float32)
    n_boxes = nx * ny // BOX**2
    xy_boxes = (
        lax.broadcasted_iota(jnp.int32, (n_boxes, nx // BOX * ny), 1) // BOX
        == lax.broadcasted_iota(jnp.int32, (n_boxes, nx // BOX * ny), 0)
    ).astype(jnp.float32)
    boxes = []
    for field in (explicit[...], -porosity_sum):
        in_x = jnp.sum(field.reshape(nx // BOX, BOX, ny, nz), axis=1)
        in_z = jnp.dot(
            in_x.reshape(nx // BOX * ny, nz),
            z_boxes,
            precision=HIGHEST,
            preferred_element_type=jnp.float32,
        )
        boxes.append(
            jnp.dot(xy_boxes, in_z, precision=HIGHEST, preferred_element_type=jnp.float32)
        )
    boxes = jnp.concatenate(boxes, axis=0)[:, : nz // BOX]
    box_row = lax.rem(lax.broadcasted_iota(jnp.int32, boxes.shape, 0), n_boxes)
    share = peers * PARAM_REGIONS
    labels = lax.broadcasted_iota(jnp.int32, (n_gx * share, nz // BOX), 0)
    found = jnp.zeros((4 * n_boxes, n_gx * share), jnp.float32)
    for b in range(n_boxes):
        y_box = b % (ny // BOX)
        region = map_ref[b // (ny // BOX), y_box : y_box + 1, :]
        found = found + lax.dot_general(
            jnp.concatenate(split_bf16(jnp.where(box_row == b, boxes, 0.0)), axis=0),
            (labels == region).astype(jnp.float32).astype(jnp.bfloat16),
            (((1,), (1,)), ((), ())),
            preferred_element_type=jnp.float32,
        )
    found = found[: 2 * n_boxes] + found[2 * n_boxes :]
    for q in range(2):
        of_q = jnp.sum(found[q * n_boxes : (q + 1) * n_boxes], axis=0, keepdims=True)
        for g in range(n_gx):
            g_s[g, q : q + 1, :] = of_q[:, g * share : (g + 1) * share]
    g_copies = []
    for offset in range(1, n_gx):
        copy = remote(
            g_s.at[lax.rem(here[0] + offset, n_gx)],
            g_r.at[offset],
            g_ss.at[offset],
            g_rs.at[offset],
            toward(0, offset),
        )
        copy.start()
        g_copies.append(copy)
    for copy in g_copies:
        copy.wait()
    part = g_s[here[0]]
    for offset in range(1, n_gx):
        part = part + g_r[offset]
    lanes = r_s.shape[2]
    together = lanes // PARAM_REGIONS
    for p in range(peers):
        first = p // together * lanes
        r_s[p] = part[:, first : first + lanes]
    r_copies = []
    for offset in range(1, peers):
        copy = remote(
            r_s.at[lax.rem(me + offset, peers)],
            r_r.at[offset],
            r_ss.at[offset],
            r_rs.at[offset],
            peer(offset),
        )
        copy.start()
        r_copies.append(copy)
    for copy in r_copies:
        copy.wait()
    part = r_s[me]
    for offset in range(1, peers):
        part = part + r_r[offset]
    mine = jnp.full((2, PARAM_REGIONS), lax.rem(me, together), jnp.int32)
    result = jnp.zeros((2, PARAM_REGIONS), jnp.float32)
    for n in range(together):
        result = jnp.where(
            mine == n, part[:, n * PARAM_REGIONS : (n + 1) * PARAM_REGIONS], result
        )
    region_ref[...] = result


def local(
    pressure,
    saturation,
    permeability,
    porosity,
    upwind_flags,
    diag_inverse,
    seismic_obs,
    well_x,
    well_y,
    well_top,
    well_len,
    well_bhp,
    well_obs,
    fault_cell,
    fault_count,
    fault_trans,
    fault_up,
    region_map,
):
    counts = tuple(lax.axis_size(axis) for axis in ("gx", "gy", "gz"))
    nx, ny, nz = permeability.shape
    peers, slots = fault_cell.shape[1:]
    wide = peers * slots
    n_wells = well_x.shape[2]
    hbm = pl.BlockSpec(memory_space=pltpu.HBM)
    vmem = pl.BlockSpec(memory_space=pltpu.VMEM)
    f32 = jnp.float32
    dma = pltpu.SemaphoreType.DMA
    faces = [(2, ny, nz), (2, nx, 1, nz), (2, ny, nz)]
    bundles = [(2, 10, ny, nz), (2, 10, nx, 1, nz), (2, 10, ny, nz)]
    lanes = 128
    share = peers * PARAM_REGIONS
    large = (
        pressure, saturation, permeability, porosity, upwind_flags, diag_inverse, seismic_obs
    )
    scratch = [
        *[pltpu.VMEM(array.shape, array.dtype) for array in large],
        dma((len(large),)),
        pltpu.VMEM((2, 3, 3, nx, ny, nz), f32),
        pltpu.VMEM((2, 3, 3, nx, ny, nz), f32),
        pltpu.VMEM((2, 3, nx, ny, nz), f32),
        pltpu.VMEM((nx, ny, nz), f32),
        pltpu.VMEM((2 * nx * ny, wide), jnp.bfloat16),
        pltpu.VMEM((nz, wide), jnp.bfloat16),
        pltpu.VMEM((8, wide), f32),
        *[pltpu.VMEM(s, f32) for s in bundles],
        *[pltpu.VMEM(s, f32) for s in bundles],
        dma((3, 2)),
        dma((3, 2)),
        pltpu.VMEM((peers, 8, slots), f32),
        pltpu.VMEM((peers, 8, slots), f32),
        dma((peers,)),
        dma((peers,)),
        pltpu.VMEM((n_wells, nz), f32),
        pltpu.VMEM((counts[2], n_wells, nz), f32),
        dma((counts[2],)),
        dma((counts[2],)),
        *[pltpu.VMEM(s, f32) for s in faces],
        *[pltpu.VMEM((2,) + s, f32) for s in faces],
        dma((3, 2)),
        dma((2, 3, 2)),
        pltpu.VMEM((peers, 1, slots), f32),
        pltpu.VMEM((2, peers, 1, slots), f32),
        dma((peers,)),
        dma((2, peers)),
        pltpu.VMEM((counts[0], 2, share), f32),
        pltpu.VMEM((counts[0], 2, share), f32),
        dma((counts[0],)),
        dma((counts[0],)),
        pltpu.VMEM((peers, 2, lanes), f32),
        pltpu.VMEM((peers, 2, lanes), f32),
        dma((peers,)),
        dma((peers,)),
    ]
    return pl.pallas_call(
        functools.partial(kernel, counts),
        out_shape=(
            jax.ShapeDtypeStruct((2, 3, nx, ny, nz), f32),
            jax.ShapeDtypeStruct((2, PARAM_REGIONS), f32),
        ),
        in_specs=[hbm] * 7 + [vmem] * 11,
        out_specs=(vmem, vmem),
        scratch_shapes=scratch,
        compiler_params=pltpu.CompilerParams(
            collective_id=0, has_side_effects=True, vmem_limit_bytes=63 * 2**20
        ),
    )(
        *large,
        well_x,
        well_y,
        well_top,
        well_len,
        well_bhp,
        well_obs,
        fault_cell,
        fault_count,
        fault_trans,
        fault_up,
        region_map,
    )


def solution(mesh):
    placed = (
        P(None, "gx", "gy", "gz"),
        P(None, None, "gx", "gy", "gz"),
        P("gx", "gy", "gz"),
        P("gx", "gy", "gz"),
        P("gx", "gy", "gz"),
        P(None, None, None, "gx", "gy", "gz"),
        P("gx", "gy", "gz"),
        P("gx", "gy", None),
        P("gx", "gy", None),
        P("gx", "gy", None),
        P("gx", "gy", None),
        P(None, "gx", "gy", None),
        P(None, "gx", "gy", None),
        P(("gx", "gy", "gz"), None, None),
        P(("gx", "gy", "gz"), None),
        P(("gx", "gy", "gz"), None, None),
        P(("gx", "gy", "gz"), None, None),
        P("gx", "gy", "gz"),
    )
    return jax.shard_map(
        local,
        mesh=mesh,
        in_specs=placed,
        out_specs=(P(None, None, "gx", "gy", "gz"), P(None, ("gx", "gy", "gz"))),
        check_vma=False,
    )
```

```python
import functools

import jax
import jax.numpy as jnp
from jax import lax
from jax.experimental import pallas as pl
from jax.experimental.pallas import tpu as pltpu
from jax.sharding import PartitionSpec as P

ITERS = 6
BOX = 4
PARAM_REGIONS = 32
MESH = pl.DeviceIdType.MESH
HIGHEST = lax.Precision.HIGHEST

fluid_viscosity = (0.4, 0.5, 1.0)
sigma_sq = 64.0


def phase_mobility(water_sat, oil_sat):
    gas_sat = 1.0 - water_sat - oil_sat
    return [
        water_sat * water_sat / fluid_viscosity[0],
        oil_sat * oil_sat / fluid_viscosity[1],
        gas_sat * gas_sat / fluid_viscosity[2],
    ]


def mobility_slopes(water_sat, oil_sat):
    gas_sat = 1.0 - water_sat - oil_sat
    return (
        2.0 * water_sat / fluid_viscosity[0] - 2.0 * gas_sat / fluid_viscosity[2],
        2.0 * oil_sat / fluid_viscosity[1] - 2.0 * gas_sat / fluid_viscosity[2],
    )


def split_bf16(value):
    high = value.astype(jnp.bfloat16)
    return high, (value - high.astype(jnp.float32)).astype(jnp.bfloat16)


def kernel(
    counts,
    pressure_hbm,
    saturation_hbm,
    perm_hbm,
    porosity_hbm,
    flags_hbm,
    inverse_hbm,
    seismic_hbm,
    well_x_ref,
    well_y_ref,
    well_top_ref,
    well_len_ref,
    bhp_ref,
    obs_ref,
    fault_cell_ref,
    fault_count_ref,
    fault_trans_ref,
    fault_up_ref,
    map_ref,
    lam_ref,
    region_ref,
    pressure_ref,
    saturation_ref,
    perm_ref,
    porosity_ref,
    flags_ref,
    inverse_ref,
    seismic_ref,
    in_sem,
    wp,
    wm,
    src,
    explicit,
    row_hot,
    z_hot,
    fault_coef,
    bx_s,
    by_s,
    bz_s,
    bx_r,
    by_r,
    bz_r,
    b_ss,
    b_rs,
    m_s,
    m_r,
    m_ss,
    m_rs,
    w_s,
    w_r,
    w_ss,
    w_rs,
    x_s,
    y_s,
    z_s,
    x_r,
    y_r,
    z_r,
    f_ss,
    f_rs,
    c_s,
    c_r,
    c_ss,
    c_rs,
    g_s,
    g_r,
    g_ss,
    g_rs,
    r_s,
    r_r,
    r_ss,
    r_rs,
):
    n_gx, n_gy, n_gz = counts
    here = (lax.axis_index("gx"), lax.axis_index("gy"), lax.axis_index("gz"))
    peers = n_gy * n_gz
    me = here[1] * n_gz + here[2]
    shape = perm_ref.shape
    nx, ny, nz = shape
    rows = nx * ny
    slots = m_r.shape[2]
    wide = peers * slots

    def toward(dim, step):
        moved = list(here)
        moved[dim] = lax.rem(here[dim] + step + counts[dim], counts[dim])
        return tuple(moved)

    def peer(offset):
        other = lax.rem(me + offset, peers)
        return (here[0], other // n_gz, lax.rem(other, n_gz))

    def remote(source, target, send, recv, device):
        return pltpu.make_async_remote_copy(
            src_ref=source,
            dst_ref=target,
            send_sem=send,
            recv_sem=recv,
            device_id=device,
            device_id_type=MESH,
        )

    loads = [
        pltpu.make_async_copy(source, target, in_sem.at[n])
        for n, (source, target) in enumerate(
            (
                (perm_hbm, perm_ref),
                (saturation_hbm, saturation_ref),
                (flags_hbm, flags_ref),
                (pressure_hbm, pressure_ref),
                (seismic_hbm, seismic_ref),
                (inverse_hbm, inverse_ref),
                (porosity_hbm, porosity_ref),
            )
        )
    ]
    for load in loads:
        load.start()
    m_r[...] = jnp.zeros_like(m_r)
    c_r[...] = jnp.zeros_like(c_r)

    barrier = pltpu.get_barrier_semaphore()
    for offset in range(1, peers):
        pl.semaphore_signal(barrier, inc=1, device_id=peer(offset), device_id_type=MESH)
    for step in range(1, n_gx):
        pl.semaphore_signal(barrier, inc=1, device_id=toward(0, step), device_id_type=MESH)
    pl.semaphore_wait(barrier, peers - 1 + n_gx - 1)
    for load in loads[:4]:
        load.wait()

    xi = lax.broadcasted_iota(jnp.int32, shape, 0)
    yi = lax.broadcasted_iota(jnp.int32, shape, 1)
    zi = lax.broadcasted_iota(jnp.int32, shape, 2)
    iotas = (xi, yi, zi)
    diagonal = xi == zi

    def pack(column):
        return jnp.sum(jnp.where(diagonal, column, 0.0), axis=0)

    def unpack(tile):
        return jnp.sum(jnp.where(diagonal, tile[None], 0.0), axis=2, keepdims=True)

    def ahead(field, dim, halo):
        if dim == 0:
            return jnp.concatenate([field[1:], halo[None]], axis=0)
        last = shape[dim] - 1
        edge = halo if dim == 1 else unpack(halo)
        return jnp.where(iotas[dim] == last, edge, pltpu.roll(field, last, dim))

    def behind(field, dim, halo):
        if dim == 0:
            return jnp.concatenate([halo[None], field[:-1]], axis=0)
        edge = halo if dim == 1 else unpack(halo)
        return jnp.where(iotas[dim] == 0, edge, pltpu.roll(field, 1, dim))

    perm = perm_ref[...]
    flags = flags_ref[...].astype(jnp.float32)
    pressure = [pressure_ref[t] for t in range(2)]
    mobility = [
        phase_mobility(saturation_ref[t + 1, 0], saturation_ref[t + 1, 1]) for t in range(2)
    ]
    bundle = [perm] + mobility[0] + mobility[1] + [flags] + pressure
    for q, field in enumerate(bundle):
        bx_s[0, q] = field[nx - 1]
        bx_s[1, q] = field[0]
        by_s[0, q] = field[:, ny - 1 :, :]
        by_s[1, q] = field[:, :1, :]
        bz_s[0, q] = pack(field[:, :, nz - 1 :])
        bz_s[1, q] = pack(field[:, :, :1])
    b_copies = []
    for dim, (sent, got) in enumerate(((bx_s, bx_r), (by_s, by_r), (bz_s, bz_r))):
        for side, step in ((0, 1), (1, -1)):
            copy = remote(
                sent.at[side],
                got.at[side],
                b_ss.at[dim, side],
                b_rs.at[dim, side],
                toward(dim, step),
            )
            copy.start()
            b_copies.append(copy)

    def as_row(ref):
        return jnp.concatenate([ref[0, p : p + 1, :] for p in range(peers)], axis=1)

    fault_cell = as_row(fault_cell_ref)
    fault_row = fault_cell // nz
    fault_z = fault_cell - fault_row * nz
    hot = (lax.broadcasted_iota(jnp.int32, (rows, wide), 0) == fault_row).astype(
        jnp.float32
    ).astype(jnp.bfloat16)
    row_hot[:rows] = hot
    row_hot[rows:] = hot
    z_hot[...] = (
        (lax.broadcasted_iota(jnp.int32, (nz, wide), 0) == fault_z)
        .astype(jnp.float32)
        .astype(jnp.bfloat16)
    )

    def gather(fields):
        stacked = []
        for field in fields:
            stacked.append(
                jnp.concatenate(split_bf16(field.reshape(rows, nz).T), axis=1)
            )
        columns = jnp.dot(
            jnp.concatenate(stacked, axis=0), row_hot[...], preferred_element_type=jnp.float32
        )
        chosen = lax.broadcasted_iota(jnp.int32, (nz, wide), 0) == fault_z
        return [
            jnp.sum(
                jnp.where(chosen, columns[k * nz : (k + 1) * nz], 0.0), axis=0, keepdims=True
            )
            for k in range(len(fields))
        ]

    own = gather(mobility[0]) + gather(mobility[1])
    for p in range(peers):
        for q in range(6):
            m_s[p, q : q + 1, :] = own[q][:, p * slots : (p + 1) * slots]
        m_s[p, 6:8, :] = jnp.zeros((2, slots), jnp.float32)
    m_copies = []
    for offset in range(1, peers):
        other = lax.rem(me + offset, peers)
        copy = remote(
            m_s.at[other], m_r.at[me], m_ss.at[offset], m_rs.at[offset], peer(offset)
        )
        copy.start()
        m_copies.append(copy)

    n_wells = well_top_ref.shape[2]
    eye = lax.broadcasted_iota(jnp.int32, (n_wells, n_wells), 0) == lax.broadcasted_iota(
        jnp.int32, (n_wells, n_wells), 1
    )

    def as_column(row):
        return jnp.sum(jnp.where(eye, row.astype(jnp.float32), 0.0), axis=1, keepdims=True)

    well_row = well_x_ref[0] * ny + well_y_ref[0]
    bhp = [as_column(bhp_ref[t, 0]) for t in range(2)]
    well_hot = (
        lax.broadcasted_iota(jnp.int32, (n_wells, rows), 1).astype(jnp.float32)
        == as_column(well_row)
    ).astype(jnp.float32)
    well_hot_t = (
        lax.broadcasted_iota(jnp.int32, (rows, n_wells), 0) == well_row
    ).astype(jnp.float32)
    depth = (here[2] * nz + lax.broadcasted_iota(jnp.int32, (n_wells, nz), 1)).astype(
        jnp.float32
    )
    top = as_column(well_top_ref[0])
    bottom = as_column(well_top_ref[0] + well_len_ref[0])
    perforated = jnp.where((depth >= top) & (depth < bottom), 1.0, 0.0)
    total = [perm * (mobility[t][0] + mobility[t][1] + mobility[t][2]) for t in range(2)]
    lane = lax.broadcasted_iota(jnp.int32, (n_wells, nz), 1)
    rates = jnp.zeros((n_wells, nz), jnp.float32)
    for t in range(2):
        with_pressure = jnp.dot(
            well_hot,
            (total[t] * pressure[t]).reshape(rows, nz),
            precision=HIGHEST,
            preferred_element_type=jnp.float32,
        )
        without = jnp.dot(
            well_hot,
            total[t].reshape(rows, nz),
            precision=HIGHEST,
            preferred_element_type=jnp.float32,
        )
        rate = jnp.sum(
            perforated * (with_pressure - bhp[t] * without), axis=1, keepdims=True
        )
        rates = jnp.where(lane == t, rate, rates)
    w_s[...] = rates
    w_copies = []
    for offset in range(1, n_gz):
        copy = remote(
            w_s, w_r.at[offset], w_ss.at[offset], w_rs.at[offset], toward(2, offset)
        )
        copy.start()
        w_copies.append(copy)

    for copy in b_copies:
        copy.wait()
    halos = ((bx_r, bx_s), (by_r, by_s), (bz_r, bz_s))
    for dim in range(3):
        got = halos[dim][0]
        up_ok = (here[dim] < counts[dim] - 1).astype(jnp.float32)
        low_ok = (here[dim] > 0).astype(jnp.float32)
        up_face = jnp.sqrt(perm * ahead(perm, dim, got[1, 0]))
        up_face = up_face * jnp.where(iotas[dim] == shape[dim] - 1, up_ok, 1.0)
        low_face = jnp.sqrt(perm * behind(perm, dim, got[0, 0]))
        low_face = low_face * jnp.where(iotas[dim] == 0, low_ok, 1.0)
        own_flags = flags.astype(jnp.int32)
        low_flags = behind(flags, dim, got[0, 7]).astype(jnp.int32)
        for t in range(2):
            bit = 3 * t + dim
            own_up = jnp.bitwise_and(jnp.right_shift(own_flags, bit), 1) == 1
            low_up = jnp.bitwise_and(jnp.right_shift(low_flags, bit), 1) == 1
            for k in range(3):
                q = 1 + 3 * t + k
                m = mobility[t][k]
                wp[t, dim, k] = up_face * jnp.where(own_up, m, ahead(m, dim, got[1, q]))
                wm[t, dim, k] = low_face * jnp.where(low_up, behind(m, dim, got[0, q]), m)

    for copy in m_copies:
        copy.wait()
    slot_index = lax.broadcasted_iota(jnp.int32, (1, slots), 1)
    scale = jnp.concatenate(
        [
            jnp.where(
                slot_index < fault_count_ref[:, p : p + 1], fault_trans_ref[0, p : p + 1, :], 0.0
            )
            for p in range(peers)
        ],
        axis=1,
    )
    fault_up = as_row(fault_up_ref)
    for t in range(2):
        own_up = jnp.bitwise_and(jnp.right_shift(fault_up, t), 1) == 1
        for k in range(3):
            q = 3 * t + k
            other = jnp.concatenate([m_r[p, q : q + 1, :] for p in range(peers)], axis=1)
            fault_coef[q : q + 1, :] = scale * jnp.where(own_up, own[q], other)

    for copy in w_copies:
        copy.wait()
    for load in loads[4:]:
        load.wait()
    rates = w_s[...]
    for offset in range(1, n_gz):
        rates = rates + w_r[offset]
    explicit_sum = jnp.zeros(shape, jnp.float32)
    for t in range(2):
        misfit = (rates[:, t : t + 1] - as_column(obs_ref[t, 0])) / sigma_sq
        weight = misfit * perforated
        spread = jnp.dot(
            well_hot_t, weight, precision=HIGHEST, preferred_element_type=jnp.float32
        ).reshape(shape)
        spread_bhp = jnp.dot(
            well_hot_t, weight * bhp[t], precision=HIGHEST, preferred_element_type=jnp.float32
        ).reshape(shape)
        drawn = pressure[t] * spread - spread_bhp
        water_slope, oil_slope = mobility_slopes(
            saturation_ref[t + 1, 0], saturation_ref[t + 1, 1]
        )
        src[t, 0] = total[t] * spread
        water_source = perm * drawn * water_slope
        if t == 1:
            water_source = water_source + saturation_ref[2, 0] - seismic_ref[...]
        src[t, 1] = water_source
        src[t, 2] = perm * drawn * oil_slope
        explicit_sum = explicit_sum + total[t] * drawn
    explicit[...] = explicit_sum

    def relax(t, coupling):
        residual = [src[t, u] for u in range(3)]
        if coupling is not None:
            residual[0] = residual[0] + coupling
        for k in range(3):
            lam_ref[t, k] = (
                inverse_ref[t, 0, k] * residual[0]
                + inverse_ref[t, 1, k] * residual[1]
                + inverse_ref[t, 2, k] * residual[2]
            )

    def face_copies(slot):
        made = []
        for dim, (sent, got) in enumerate(((x_s, x_r), (y_s, y_r), (z_s, z_r))):
            for side, step in ((0, 1), (1, -1)):
                made.append(
                    remote(
                        sent.at[side],
                        got.at[slot, side],
                        f_ss.at[dim, side],
                        f_rs.at[slot, dim, side],
                        toward(dim, step),
                    )
                )
        return made

    def products(t):
        lam = [lam_ref[t, k] for k in range(3)]
        up = []
        down = []
        for dim in range(3):
            up.append(sum(wp[t, dim, k] * lam[k] for k in range(3)))
            down.append(sum(wm[t, dim, k] * lam[k] for k in range(3)))
        x_s[0] = up[0][nx - 1]
        x_s[1] = down[0][0]
        y_s[0] = up[1][:, ny - 1 :, :]
        y_s[1] = down[1][:, :1, :]
        z_s[0] = pack(up[2][:, :, nz - 1 :])
        z_s[1] = pack(down[2][:, :, :1])
        return lam, up, down

    def terms(up, down, slot):
        faces = (x_r, y_r, z_r)
        upper = [ahead(down[dim], dim, faces[dim][slot, 1]) for dim in range(3)]
        lower = [behind(up[dim], dim, faces[dim][slot, 0]) for dim in range(3)]
        return upper, lower

    def sweep(t, n_face, n_fault):
        face_slot = lax.rem(n_face, 2)
        slot = lax.rem(n_fault, 2)
        values = gather([lam_ref[t, k] for k in range(3)])
        sent = sum(
            fault_coef[3 * t + k : 3 * t + k + 1, :] * values[k] for k in range(3)
        )
        for p in range(peers):
            c_s[p] = sent[:, p * slots : (p + 1) * slots]
        copies = []
        for offset in range(1, peers):
            other = lax.rem(me + offset, peers)
            copy = remote(
                c_s.at[other],
                c_r.at[slot, me],
                c_ss.at[offset],
                c_rs.at[slot, offset],
                peer(offset),
            )
            copy.start()
            copies.append(copy)
        lam, up, down = products(t)
        faces = face_copies(face_slot)
        for copy in faces:
            copy.start()
        for copy in faces:
            copy.wait()
        upper, lower = terms(up, down, face_slot)
        coupling = upper[0] + lower[0] + upper[1] + lower[1] + upper[2] + lower[2]
        for copy in copies:
            copy.wait()
        arrived = jnp.concatenate([c_r[slot, p] for p in range(peers)], axis=1)
        picked = jnp.where(
            lax.broadcasted_iota(jnp.int32, (rows, wide), 0) == fault_row, arrived, 0.0
        )
        both = jnp.concatenate(split_bf16(picked), axis=0)
        added = lax.dot_general(
            both,
            z_hot[...],
            (((1,), (1,)), ((), ())),
            preferred_element_type=jnp.float32,
        )
        coupling = coupling + (added[:rows] + added[rows:]).reshape(shape)
        relax(t, coupling)

    log_perm = explicit_sum
    for turn, t in enumerate((1, 0)):
        if t == 1:
            relax(1, None)

        def body(step, carry, t=t, turn=turn):
            sweep(t, turn * ITERS + step, turn * (ITERS - 1) + step)
            return carry

        lax.fori_loop(0, ITERS - 1, body, 0)
        slot = (turn * ITERS + ITERS - 1) % 2
        lam, up, down = products(t)
        faces = face_copies(slot)
        for copy in faces:
            copy.start()
        if t == 0:
            porosity_sum = jnp.zeros(shape, jnp.float32)
            for at in range(2):
                water = saturation_ref[at + 1, 0] - saturation_ref[at, 0]
                oil = saturation_ref[at + 1, 1] - saturation_ref[at, 1]
                porosity_sum = porosity_sum + (
                    lam_ref[at, 0] * water + lam_ref[at, 1] * oil - lam_ref[at, 2] * (water + oil)
                )
        else:
            porosity = porosity_ref[...]
            src[0, 1] += porosity * (lam[0] - lam[2])
            src[0, 2] += porosity * (lam[1] - lam[2])
            relax(0, None)
        for copy in faces:
            copy.wait()
        upper, lower = terms(up, down, slot)
        p_here = pressure_ref[t]
        flux = jnp.zeros(shape, jnp.float32)
        for dim in range(3):
            got = halos[dim][0]
            flux = (
                flux
                + 0.5
                * (p_here - ahead(p_here, dim, got[1, 8 + t]))
                * (up[dim] - upper[dim])
                + 0.5
                * (behind(p_here, dim, got[0, 8 + t]) - p_here)
                * (lower[dim] - down[dim])
            )
        explicit[...] -= flux

    z_boxes = (
        lax.broadcasted_iota(jnp.int32, (nz, nz), 0) // BOX
        == lax.broadcasted_iota(jnp.int32, (nz, nz), 1)
    ).astype(jnp.float32)
    n_boxes = nx * ny // BOX**2
    xy_boxes = (
        lax.broadcasted_iota(jnp.int32, (n_boxes, nx // BOX * ny), 1) // BOX
        == lax.broadcasted_iota(jnp.int32, (n_boxes, nx // BOX * ny), 0)
    ).astype(jnp.float32)
    boxes = []
    for field in (explicit[...], -porosity_sum):
        in_x = jnp.sum(field.reshape(nx // BOX, BOX, ny, nz), axis=1)
        in_z = jnp.dot(
            in_x.reshape(nx // BOX * ny, nz),
            z_boxes,
            precision=HIGHEST,
            preferred_element_type=jnp.float32,
        )
        boxes.append(
            jnp.dot(xy_boxes, in_z, precision=HIGHEST, preferred_element_type=jnp.float32)
        )
    boxes = jnp.concatenate(boxes, axis=0)[:, : nz // BOX]
    box_row = lax.rem(lax.broadcasted_iota(jnp.int32, boxes.shape, 0), n_boxes)
    share = peers * PARAM_REGIONS
    labels = lax.broadcasted_iota(jnp.int32, (n_gx * share, nz // BOX), 0)
    found = jnp.zeros((4 * n_boxes, n_gx * share), jnp.float32)
    for b in range(n_boxes):
        y_box = b % (ny // BOX)
        region = map_ref[b // (ny // BOX), y_box : y_box + 1, :]
        found = found + lax.dot_general(
            jnp.concatenate(split_bf16(jnp.where(box_row == b, boxes, 0.0)), axis=0),
            (labels == region).astype(jnp.float32).astype(jnp.bfloat16),
            (((1,), (1,)), ((), ())),
            preferred_element_type=jnp.float32,
        )
    found = found[: 2 * n_boxes] + found[2 * n_boxes :]
    for q in range(2):
        of_q = jnp.sum(found[q * n_boxes : (q + 1) * n_boxes], axis=0, keepdims=True)
        for g in range(n_gx):
            g_s[g, q : q + 1, :] = of_q[:, g * share : (g + 1) * share]
    g_copies = []
    for offset in range(1, n_gx):
        copy = remote(
            g_s.at[lax.rem(here[0] + offset, n_gx)],
            g_r.at[offset],
            g_ss.at[offset],
            g_rs.at[offset],
            toward(0, offset),
        )
        copy.start()
        g_copies.append(copy)
    for copy in g_copies:
        copy.wait()
    part = g_s[here[0]]
    for offset in range(1, n_gx):
        part = part + g_r[offset]
    lanes = r_s.shape[2]
    together = lanes // PARAM_REGIONS
    for p in range(peers):
        first = p // together * lanes
        r_s[p] = part[:, first : first + lanes]
    r_copies = []
    for offset in range(1, peers):
        copy = remote(
            r_s.at[lax.rem(me + offset, peers)],
            r_r.at[offset],
            r_ss.at[offset],
            r_rs.at[offset],
            peer(offset),
        )
        copy.start()
        r_copies.append(copy)
    for copy in r_copies:
        copy.wait()
    part = r_s[me]
    for offset in range(1, peers):
        part = part + r_r[offset]
    mine = jnp.full((2, PARAM_REGIONS), lax.rem(me, together), jnp.int32)
    result = jnp.zeros((2, PARAM_REGIONS), jnp.float32)
    for n in range(together):
        result = jnp.where(
            mine == n, part[:, n * PARAM_REGIONS : (n + 1) * PARAM_REGIONS], result
        )
    region_ref[...] = result


def local(
    pressure,
    saturation,
    permeability,
    porosity,
    upwind_flags,
    diag_inverse,
    seismic_obs,
    well_x,
    well_y,
    well_top,
    well_len,
    well_bhp,
    well_obs,
    fault_cell,
    fault_count,
    fault_trans,
    fault_up,
    region_map,
):
    counts = tuple(lax.axis_size(axis) for axis in ("gx", "gy", "gz"))
    nx, ny, nz = permeability.shape
    peers, slots = fault_cell.shape[1:]
    wide = peers * slots
    n_wells = well_x.shape[2]
    hbm = pl.BlockSpec(memory_space=pltpu.HBM)
    vmem = pl.BlockSpec(memory_space=pltpu.VMEM)
    f32 = jnp.float32
    dma = pltpu.SemaphoreType.DMA
    faces = [(2, ny, nz), (2, nx, 1, nz), (2, ny, nz)]
    bundles = [(2, 10, ny, nz), (2, 10, nx, 1, nz), (2, 10, ny, nz)]
    lanes = 128
    share = peers * PARAM_REGIONS
    large = (
        pressure, saturation, permeability, porosity, upwind_flags, diag_inverse, seismic_obs
    )
    scratch = [
        *[pltpu.VMEM(array.shape, array.dtype) for array in large],
        dma((len(large),)),
        pltpu.VMEM((2, 3, 3, nx, ny, nz), f32),
        pltpu.VMEM((2, 3, 3, nx, ny, nz), f32),
        pltpu.VMEM((2, 3, nx, ny, nz), f32),
        pltpu.VMEM((nx, ny, nz), f32),
        pltpu.VMEM((2 * nx * ny, wide), jnp.bfloat16),
        pltpu.VMEM((nz, wide), jnp.bfloat16),
        pltpu.VMEM((8, wide), f32),
        *[pltpu.VMEM(s, f32) for s in bundles],
        *[pltpu.VMEM(s, f32) for s in bundles],
        dma((3, 2)),
        dma((3, 2)),
        pltpu.VMEM((peers, 8, slots), f32),
        pltpu.VMEM((peers, 8, slots), f32),
        dma((peers,)),
        dma((peers,)),
        pltpu.VMEM((n_wells, nz), f32),
        pltpu.VMEM((counts[2], n_wells, nz), f32),
        dma((counts[2],)),
        dma((counts[2],)),
        *[pltpu.VMEM(s, f32) for s in faces],
        *[pltpu.VMEM((2,) + s, f32) for s in faces],
        dma((3, 2)),
        dma((2, 3, 2)),
        pltpu.VMEM((peers, 1, slots), f32),
        pltpu.VMEM((2, peers, 1, slots), f32),
        dma((peers,)),
        dma((2, peers)),
        pltpu.VMEM((counts[0], 2, share), f32),
        pltpu.VMEM((counts[0], 2, share), f32),
        dma((counts[0],)),
        dma((counts[0],)),
        pltpu.VMEM((peers, 2, lanes), f32),
        pltpu.VMEM((peers, 2, lanes), f32),
        dma((peers,)),
        dma((peers,)),
    ]
    return pl.pallas_call(
        functools.partial(kernel, counts),
        out_shape=(
            jax.ShapeDtypeStruct((2, 3, nx, ny, nz), f32),
            jax.ShapeDtypeStruct((2, PARAM_REGIONS), f32),
        ),
        in_specs=[hbm] * 7 + [vmem] * 11,
        out_specs=(vmem, vmem),
        scratch_shapes=scratch,
        compiler_params=pltpu.CompilerParams(
            collective_id=0, has_side_effects=True, vmem_limit_bytes=63 * 2**20
        ),
    )(
        *large,
        well_x,
        well_y,
        well_top,
        well_len,
        well_bhp,
        well_obs,
        fault_cell,
        fault_count,
        fault_trans,
        fault_up,
        region_map,
    )


def solution(mesh):
    placed = (
        P(None, "gx", "gy", "gz"),
        P(None, None, "gx", "gy", "gz"),
        P("gx", "gy", "gz"),
        P("gx", "gy", "gz"),
        P("gx", "gy", "gz"),
        P(None, None, None, "gx", "gy", "gz"),
        P("gx", "gy", "gz"),
        P("gx", "gy", None),
        P("gx", "gy", None),
        P("gx", "gy", None),
        P("gx", "gy", None),
        P(None, "gx", "gy", None),
        P(None, "gx", "gy", None),
        P(("gx", "gy", "gz"), None, None),
        P(("gx", "gy", "gz"), None),
        P(("gx", "gy", "gz"), None, None),
        P(("gx", "gy", "gz"), None, None),
        P("gx", "gy", "gz"),
    )
    return jax.shard_map(
        local,
        mesh=mesh,
        in_specs=placed,
        out_specs=(P(None, None, "gx", "gy", "gz"), P(None, ("gx", "gy", "gz"))),
        check_vma=False,
    )
```

```python
import functools

import jax
import jax.numpy as jnp
from jax import lax
from jax.experimental import pallas as pl
from jax.experimental.pallas import tpu as pltpu
from jax.sharding import PartitionSpec as P

ITERS = 6
BOX = 4
PARAM_REGIONS = 32
MESH = pl.DeviceIdType.MESH
HIGHEST = lax.Precision.HIGHEST

fluid_viscosity = (0.4, 0.5, 1.0)
sigma_sq = 64.0


def phase_mobility(water_sat, oil_sat):
    gas_sat = 1.0 - water_sat - oil_sat
    return [
        water_sat * water_sat / fluid_viscosity[0],
        oil_sat * oil_sat / fluid_viscosity[1],
        gas_sat * gas_sat / fluid_viscosity[2],
    ]


def mobility_slopes(water_sat, oil_sat):
    gas_sat = 1.0 - water_sat - oil_sat
    return (
        2.0 * water_sat / fluid_viscosity[0] - 2.0 * gas_sat / fluid_viscosity[2],
        2.0 * oil_sat / fluid_viscosity[1] - 2.0 * gas_sat / fluid_viscosity[2],
    )


def split_bf16(value):
    high = value.astype(jnp.bfloat16)
    return high, (value - high.astype(jnp.float32)).astype(jnp.bfloat16)


def kernel(
    counts,
    pressure_hbm,
    saturation_hbm,
    perm_hbm,
    porosity_hbm,
    flags_hbm,
    inverse_hbm,
    seismic_hbm,
    well_x_ref,
    well_y_ref,
    well_top_ref,
    well_len_ref,
    bhp_ref,
    obs_ref,
    fault_cell_ref,
    fault_count_ref,
    fault_trans_ref,
    fault_up_ref,
    map_ref,
    lam_ref,
    region_ref,
    pressure_ref,
    saturation_ref,
    perm_ref,
    porosity_ref,
    flags_ref,
    inverse_ref,
    seismic_ref,
    in_sem,
    wp,
    wm,
    src,
    explicit,
    row_hot,
    z_hot,
    fault_coef,
    bx_s,
    by_s,
    bz_s,
    bx_r,
    by_r,
    bz_r,
    b_ss,
    b_rs,
    m_s,
    m_r,
    m_ss,
    m_rs,
    w_s,
    w_r,
    w_ss,
    w_rs,
    x_s,
    y_s,
    z_s,
    x_r,
    y_r,
    z_r,
    f_ss,
    f_rs,
    c_s,
    c_r,
    c_ss,
    c_rs,
    g_s,
    g_r,
    g_ss,
    g_rs,
    r_s,
    r_r,
    r_ss,
    r_rs,
):
    n_gx, n_gy, n_gz = counts
    here = (lax.axis_index("gx"), lax.axis_index("gy"), lax.axis_index("gz"))
    peers = n_gy * n_gz
    me = here[1] * n_gz + here[2]
    shape = perm_ref.shape
    nx, ny, nz = shape
    rows = nx * ny
    slots = m_r.shape[2]
    wide = peers * slots

    def toward(dim, step):
        moved = list(here)
        moved[dim] = lax.rem(here[dim] + step + counts[dim], counts[dim])
        return tuple(moved)

    def peer(offset):
        other = lax.rem(me + offset, peers)
        return (here[0], other // n_gz, lax.rem(other, n_gz))

    def remote(source, target, send, recv, device):
        return pltpu.make_async_remote_copy(
            src_ref=source,
            dst_ref=target,
            send_sem=send,
            recv_sem=recv,
            device_id=device,
            device_id_type=MESH,
        )

    loads = [
        pltpu.make_async_copy(source, target, in_sem.at[n])
        for n, (source, target) in enumerate(
            (
                (perm_hbm, perm_ref),
                (saturation_hbm, saturation_ref),
                (flags_hbm, flags_ref),
                (pressure_hbm, pressure_ref),
                (seismic_hbm, seismic_ref),
                (inverse_hbm, inverse_ref),
                (porosity_hbm, porosity_ref),
            )
        )
    ]
    for load in loads:
        load.start()
    m_r[...] = jnp.zeros_like(m_r)
    c_r[...] = jnp.zeros_like(c_r)

    barrier = pltpu.get_barrier_semaphore()
    for offset in range(1, peers):
        pl.semaphore_signal(barrier, inc=1, device_id=peer(offset), device_id_type=MESH)
    for step in range(1, n_gx):
        pl.semaphore_signal(barrier, inc=1, device_id=toward(0, step), device_id_type=MESH)
    pl.semaphore_wait(barrier, peers - 1 + n_gx - 1)
    for load in loads[:4]:
        load.wait()

    xi = lax.broadcasted_iota(jnp.int32, shape, 0)
    yi = lax.broadcasted_iota(jnp.int32, shape, 1)
    zi = lax.broadcasted_iota(jnp.int32, shape, 2)
    iotas = (xi, yi, zi)
    diagonal = xi == zi

    def pack(column):
        return jnp.sum(jnp.where(diagonal, column, 0.0), axis=0)

    def unpack(tile):
        return jnp.sum(jnp.where(diagonal, tile[None], 0.0), axis=2, keepdims=True)

    def ahead(field, dim, halo):
        if dim == 0:
            return jnp.concatenate([field[1:], halo[None]], axis=0)
        last = shape[dim] - 1
        edge = halo if dim == 1 else unpack(halo)
        return jnp.where(iotas[dim] == last, edge, pltpu.roll(field, last, dim))

    def behind(field, dim, halo):
        if dim == 0:
            return jnp.concatenate([halo[None], field[:-1]], axis=0)
        edge = halo if dim == 1 else unpack(halo)
        return jnp.where(iotas[dim] == 0, edge, pltpu.roll(field, 1, dim))

    perm = perm_ref[...]
    flags = flags_ref[...].astype(jnp.float32)
    pressure = [pressure_ref[t] for t in range(2)]
    mobility = [
        phase_mobility(saturation_ref[t + 1, 0], saturation_ref[t + 1, 1]) for t in range(2)
    ]
    bundle = [perm] + mobility[0] + mobility[1] + [flags] + pressure
    for q, field in enumerate(bundle):
        bx_s[0, q] = field[nx - 1]
        bx_s[1, q] = field[0]
        by_s[0, q] = field[:, ny - 1 :, :]
        by_s[1, q] = field[:, :1, :]
        bz_s[0, q] = pack(field[:, :, nz - 1 :])
        bz_s[1, q] = pack(field[:, :, :1])
    b_copies = []
    for dim, (sent, got) in enumerate(((bx_s, bx_r), (by_s, by_r), (bz_s, bz_r))):
        for side, step in ((0, 1), (1, -1)):
            copy = remote(
                sent.at[side],
                got.at[side],
                b_ss.at[dim, side],
                b_rs.at[dim, side],
                toward(dim, step),
            )
            copy.start()
            b_copies.append(copy)

    def as_row(ref):
        return jnp.concatenate([ref[0, p : p + 1, :] for p in range(peers)], axis=1)

    fault_cell = as_row(fault_cell_ref)
    fault_row = fault_cell // nz
    fault_z = fault_cell - fault_row * nz
    hot = (lax.broadcasted_iota(jnp.int32, (rows, wide), 0) == fault_row).astype(
        jnp.float32
    ).astype(jnp.bfloat16)
    row_hot[:rows] = hot
    row_hot[rows:] = hot
    z_hot[...] = (
        (lax.broadcasted_iota(jnp.int32, (nz, wide), 0) == fault_z)
        .astype(jnp.float32)
        .astype(jnp.bfloat16)
    )

    def gather(fields):
        stacked = []
        for field in fields:
            stacked.append(
                jnp.concatenate(split_bf16(field.reshape(rows, nz).T), axis=1)
            )
        columns = jnp.dot(
            jnp.concatenate(stacked, axis=0), row_hot[...], preferred_element_type=jnp.float32
        )
        chosen = lax.broadcasted_iota(jnp.int32, (nz, wide), 0) == fault_z
        return [
            jnp.sum(
                jnp.where(chosen, columns[k * nz : (k + 1) * nz], 0.0), axis=0, keepdims=True
            )
            for k in range(len(fields))
        ]

    own = gather(mobility[0]) + gather(mobility[1])
    for p in range(peers):
        for q in range(6):
            m_s[p, q : q + 1, :] = own[q][:, p * slots : (p + 1) * slots]
        m_s[p, 6:8, :] = jnp.zeros((2, slots), jnp.float32)
    m_copies = []
    for offset in range(1, peers):
        other = lax.rem(me + offset, peers)
        copy = remote(
            m_s.at[other], m_r.at[me], m_ss.at[offset], m_rs.at[offset], peer(offset)
        )
        copy.start()
        m_copies.append(copy)

    n_wells = well_top_ref.shape[2]
    eye = lax.broadcasted_iota(jnp.int32, (n_wells, n_wells), 0) == lax.broadcasted_iota(
        jnp.int32, (n_wells, n_wells), 1
    )

    def as_column(row):
        return jnp.sum(jnp.where(eye, row.astype(jnp.float32), 0.0), axis=1, keepdims=True)

    well_row = well_x_ref[0] * ny + well_y_ref[0]
    bhp = [as_column(bhp_ref[t, 0]) for t in range(2)]
    well_hot = (
        lax.broadcasted_iota(jnp.int32, (n_wells, rows), 1).astype(jnp.float32)
        == as_column(well_row)
    ).astype(jnp.float32)
    well_hot_t = (
        lax.broadcasted_iota(jnp.int32, (rows, n_wells), 0) == well_row
    ).astype(jnp.float32)
    depth = (here[2] * nz + lax.broadcasted_iota(jnp.int32, (n_wells, nz), 1)).astype(
        jnp.float32
    )
    top = as_column(well_top_ref[0])
    bottom = as_column(well_top_ref[0] + well_len_ref[0])
    perforated = jnp.where((depth >= top) & (depth < bottom), 1.0, 0.0)
    total = [perm * (mobility[t][0] + mobility[t][1] + mobility[t][2]) for t in range(2)]
    lane = lax.broadcasted_iota(jnp.int32, (n_wells, nz), 1)
    rates = jnp.zeros((n_wells, nz), jnp.float32)
    for t in range(2):
        with_pressure = jnp.dot(
            well_hot,
            (total[t] * pressure[t]).reshape(rows, nz),
            precision=HIGHEST,
            preferred_element_type=jnp.float32,
        )
        without = jnp.dot(
            well_hot,
            total[t].reshape(rows, nz),
            precision=HIGHEST,
            preferred_element_type=jnp.float32,
        )
        rate = jnp.sum(
            perforated * (with_pressure - bhp[t] * without), axis=1, keepdims=True
        )
        rates = jnp.where(lane == t, rate, rates)
    w_s[...] = rates
    w_copies = []
    for offset in range(1, n_gz):
        copy = remote(
            w_s, w_r.at[offset], w_ss.at[offset], w_rs.at[offset], toward(2, offset)
        )
        copy.start()
        w_copies.append(copy)

    for copy in b_copies:
        copy.wait()
    halos = ((bx_r, bx_s), (by_r, by_s), (bz_r, bz_s))
    for dim in range(3):
        got = halos[dim][0]
        up_ok = (here[dim] < counts[dim] - 1).astype(jnp.float32)
        low_ok = (here[dim] > 0).astype(jnp.float32)
        up_face = jnp.sqrt(perm * ahead(perm, dim, got[1, 0]))
        up_face = up_face * jnp.where(iotas[dim] == shape[dim] - 1, up_ok, 1.0)
        low_face = jnp.sqrt(perm * behind(perm, dim, got[0, 0]))
        low_face = low_face * jnp.where(iotas[dim] == 0, low_ok, 1.0)
        own_flags = flags.astype(jnp.int32)
        low_flags = behind(flags, dim, got[0, 7]).astype(jnp.int32)
        for t in range(2):
            bit = 3 * t + dim
            own_up = jnp.bitwise_and(jnp.right_shift(own_flags, bit), 1) == 1
            low_up = jnp.bitwise_and(jnp.right_shift(low_flags, bit), 1) == 1
            for k in range(3):
                q = 1 + 3 * t + k
                m = mobility[t][k]
                wp[t, dim, k] = up_face * jnp.where(own_up, m, ahead(m, dim, got[1, q]))
                wm[t, dim, k] = low_face * jnp.where(low_up, behind(m, dim, got[0, q]), m)

    for copy in m_copies:
        copy.wait()
    slot_index = lax.broadcasted_iota(jnp.int32, (1, slots), 1)
    scale = jnp.concatenate(
        [
            jnp.where(
                slot_index < fault_count_ref[:, p : p + 1], fault_trans_ref[0, p : p + 1, :], 0.0
            )
            for p in range(peers)
        ],
        axis=1,
    )
    fault_up = as_row(fault_up_ref)
    for t in range(2):
        own_up = jnp.bitwise_and(jnp.right_shift(fault_up, t), 1) == 1
        for k in range(3):
            q = 3 * t + k
            other = jnp.concatenate([m_r[p, q : q + 1, :] for p in range(peers)], axis=1)
            fault_coef[q : q + 1, :] = scale * jnp.where(own_up, own[q], other)

    for copy in w_copies:
        copy.wait()
    for load in loads[4:]:
        load.wait()
    rates = w_s[...]
    for offset in range(1, n_gz):
        rates = rates + w_r[offset]
    explicit_sum = jnp.zeros(shape, jnp.float32)
    for t in range(2):
        misfit = (rates[:, t : t + 1] - as_column(obs_ref[t, 0])) / sigma_sq
        weight = misfit * perforated
        spread = jnp.dot(
            well_hot_t, weight, precision=HIGHEST, preferred_element_type=jnp.float32
        ).reshape(shape)
        spread_bhp = jnp.dot(
            well_hot_t, weight * bhp[t], precision=HIGHEST, preferred_element_type=jnp.float32
        ).reshape(shape)
        drawn = pressure[t] * spread - spread_bhp
        water_slope, oil_slope = mobility_slopes(
            saturation_ref[t + 1, 0], saturation_ref[t + 1, 1]
        )
        src[t, 0] = total[t] * spread
        water_source = perm * drawn * water_slope
        if t == 1:
            water_source = water_source + saturation_ref[2, 0] - seismic_ref[...]
        src[t, 1] = water_source
        src[t, 2] = perm * drawn * oil_slope
        explicit_sum = explicit_sum + total[t] * drawn
    explicit[...] = explicit_sum

    def relax(t, coupling):
        residual = [src[t, u] for u in range(3)]
        if coupling is not None:
            residual[0] = residual[0] + coupling
        for k in range(3):
            lam_ref[t, k] = (
                inverse_ref[t, 0, k] * residual[0]
                + inverse_ref[t, 1, k] * residual[1]
                + inverse_ref[t, 2, k] * residual[2]
            )

    def face_copies(slot):
        made = []
        for dim, (sent, got) in enumerate(((x_s, x_r), (y_s, y_r), (z_s, z_r))):
            for side, step in ((0, 1), (1, -1)):
                made.append(
                    remote(
                        sent.at[side],
                        got.at[slot, side],
                        f_ss.at[dim, side],
                        f_rs.at[slot, dim, side],
                        toward(dim, step),
                    )
                )
        return made

    def products(t):
        lam = [lam_ref[t, k] for k in range(3)]
        up = []
        down = []
        for dim in range(3):
            up.append(sum(wp[t, dim, k] * lam[k] for k in range(3)))
            down.append(sum(wm[t, dim, k] * lam[k] for k in range(3)))
        x_s[0] = up[0][nx - 1]
        x_s[1] = down[0][0]
        y_s[0] = up[1][:, ny - 1 :, :]
        y_s[1] = down[1][:, :1, :]
        z_s[0] = pack(up[2][:, :, nz - 1 :])
        z_s[1] = pack(down[2][:, :, :1])
        return lam, up, down

    def terms(up, down, slot):
        faces = (x_r, y_r, z_r)
        upper = [ahead(down[dim], dim, faces[dim][slot, 1]) for dim in range(3)]
        lower = [behind(up[dim], dim, faces[dim][slot, 0]) for dim in range(3)]
        return upper, lower

    def sweep(t, n_face, n_fault):
        face_slot = lax.rem(n_face, 2)
        slot = lax.rem(n_fault, 2)
        values = gather([lam_ref[t, k] for k in range(3)])
        sent = sum(
            fault_coef[3 * t + k : 3 * t + k + 1, :] * values[k] for k in range(3)
        )
        for p in range(peers):
            c_s[p] = sent[:, p * slots : (p + 1) * slots]
        copies = []
        for offset in range(1, peers):
            other = lax.rem(me + offset, peers)
            copy = remote(
                c_s.at[other],
                c_r.at[slot, me],
                c_ss.at[offset],
                c_rs.at[slot, offset],
                peer(offset),
            )
            copy.start()
            copies.append(copy)
        lam, up, down = products(t)
        faces = face_copies(face_slot)
        for copy in faces:
            copy.start()
        for copy in faces:
            copy.wait()
        upper, lower = terms(up, down, face_slot)
        coupling = upper[0] + lower[0] + upper[1] + lower[1] + upper[2] + lower[2]
        for copy in copies:
            copy.wait()
        arrived = jnp.concatenate([c_r[slot, p] for p in range(peers)], axis=1)
        hot = row_hot[:rows]
        both = jnp.concatenate(
            [hot * jnp.broadcast_to(part, hot.shape) for part in split_bf16(arrived)], axis=0
        )
        added = lax.dot_general(
            both,
            z_hot[...],
            (((1,), (1,)), ((), ())),
            preferred_element_type=jnp.float32,
        )
        coupling = coupling + (added[:rows] + added[rows:]).reshape(shape)
        relax(t, coupling)

    log_perm = explicit_sum
    for turn, t in enumerate((1, 0)):
        if t == 1:
            relax(1, None)

        def body(step, carry, t=t, turn=turn):
            sweep(t, turn * ITERS + step, turn * (ITERS - 1) + step)
            return carry

        lax.fori_loop(0, ITERS - 1, body, 0)
        slot = (turn * ITERS + ITERS - 1) % 2
        lam, up, down = products(t)
        faces = face_copies(slot)
        for copy in faces:
            copy.start()
        if t == 0:
            porosity_sum = jnp.zeros(shape, jnp.float32)
            for at in range(2):
                water = saturation_ref[at + 1, 0] - saturation_ref[at, 0]
                oil = saturation_ref[at + 1, 1] - saturation_ref[at, 1]
                porosity_sum = porosity_sum + (
                    lam_ref[at, 0] * water + lam_ref[at, 1] * oil - lam_ref[at, 2] * (water + oil)
                )
        else:
            porosity = porosity_ref[...]
            src[0, 1] += porosity * (lam[0] - lam[2])
            src[0, 2] += porosity * (lam[1] - lam[2])
            relax(0, None)
        for copy in faces:
            copy.wait()
        upper, lower = terms(up, down, slot)
        p_here = pressure_ref[t]
        flux = jnp.zeros(shape, jnp.float32)
        for dim in range(3):
            got = halos[dim][0]
            flux = (
                flux
                + 0.5
                * (p_here - ahead(p_here, dim, got[1, 8 + t]))
                * (up[dim] - upper[dim])
                + 0.5
                * (behind(p_here, dim, got[0, 8 + t]) - p_here)
                * (lower[dim] - down[dim])
            )
        explicit[...] -= flux

    z_boxes = (
        lax.broadcasted_iota(jnp.int32, (nz, nz), 0) // BOX
        == lax.broadcasted_iota(jnp.int32, (nz, nz), 1)
    ).astype(jnp.float32)
    n_boxes = nx * ny // BOX**2
    xy_boxes = (
        lax.broadcasted_iota(jnp.int32, (n_boxes, nx // BOX * ny), 1) // BOX
        == lax.broadcasted_iota(jnp.int32, (n_boxes, nx // BOX * ny), 0)
    ).astype(jnp.float32)
    boxes = []
    for field in (explicit[...], -porosity_sum):
        in_x = jnp.sum(field.reshape(nx // BOX, BOX, ny, nz), axis=1)
        in_z = jnp.dot(
            in_x.reshape(nx // BOX * ny, nz),
            z_boxes,
            precision=HIGHEST,
            preferred_element_type=jnp.float32,
        )
        boxes.append(
            jnp.dot(xy_boxes, in_z, precision=HIGHEST, preferred_element_type=jnp.float32)
        )
    boxes = jnp.concatenate(boxes, axis=0)[:, : nz // BOX]
    box_row = lax.rem(lax.broadcasted_iota(jnp.int32, boxes.shape, 0), n_boxes)
    share = peers * PARAM_REGIONS
    labels = lax.broadcasted_iota(jnp.int32, (n_gx * share, nz // BOX), 0)
    found = jnp.zeros((4 * n_boxes, n_gx * share), jnp.float32)
    for b in range(n_boxes):
        y_box = b % (ny // BOX)
        region = map_ref[b // (ny // BOX), y_box : y_box + 1, :]
        found = found + lax.dot_general(
            jnp.concatenate(split_bf16(jnp.where(box_row == b, boxes, 0.0)), axis=0),
            (labels == region).astype(jnp.float32).astype(jnp.bfloat16),
            (((1,), (1,)), ((), ())),
            preferred_element_type=jnp.float32,
        )
    found = found[: 2 * n_boxes] + found[2 * n_boxes :]
    for q in range(2):
        of_q = jnp.sum(found[q * n_boxes : (q + 1) * n_boxes], axis=0, keepdims=True)
        for g in range(n_gx):
            g_s[g, q : q + 1, :] = of_q[:, g * share : (g + 1) * share]
    g_copies = []
    for offset in range(1, n_gx):
        copy = remote(
            g_s.at[lax.rem(here[0] + offset, n_gx)],
            g_r.at[offset],
            g_ss.at[offset],
            g_rs.at[offset],
            toward(0, offset),
        )
        copy.start()
        g_copies.append(copy)
    for copy in g_copies:
        copy.wait()
    part = g_s[here[0]]
    for offset in range(1, n_gx):
        part = part + g_r[offset]
    lanes = r_s.shape[2]
    together = lanes // PARAM_REGIONS
    for p in range(peers):
        first = p // together * lanes
        r_s[p] = part[:, first : first + lanes]
    r_copies = []
    for offset in range(1, peers):
        copy = remote(
            r_s.at[lax.rem(me + offset, peers)],
            r_r.at[offset],
            r_ss.at[offset],
            r_rs.at[offset],
            peer(offset),
        )
        copy.start()
        r_copies.append(copy)
    for copy in r_copies:
        copy.wait()
    part = r_s[me]
    for offset in range(1, peers):
        part = part + r_r[offset]
    mine = jnp.full((2, PARAM_REGIONS), lax.rem(me, together), jnp.int32)
    result = jnp.zeros((2, PARAM_REGIONS), jnp.float32)
    for n in range(together):
        result = jnp.where(
            mine == n, part[:, n * PARAM_REGIONS : (n + 1) * PARAM_REGIONS], result
        )
    region_ref[...] = result


def local(
    pressure,
    saturation,
    permeability,
    porosity,
    upwind_flags,
    diag_inverse,
    seismic_obs,
    well_x,
    well_y,
    well_top,
    well_len,
    well_bhp,
    well_obs,
    fault_cell,
    fault_count,
    fault_trans,
    fault_up,
    region_map,
):
    counts = tuple(lax.axis_size(axis) for axis in ("gx", "gy", "gz"))
    nx, ny, nz = permeability.shape
    peers, slots = fault_cell.shape[1:]
    wide = peers * slots
    n_wells = well_x.shape[2]
    hbm = pl.BlockSpec(memory_space=pltpu.HBM)
    vmem = pl.BlockSpec(memory_space=pltpu.VMEM)
    f32 = jnp.float32
    dma = pltpu.SemaphoreType.DMA
    faces = [(2, ny, nz), (2, nx, 1, nz), (2, ny, nz)]
    bundles = [(2, 10, ny, nz), (2, 10, nx, 1, nz), (2, 10, ny, nz)]
    lanes = 128
    share = peers * PARAM_REGIONS
    large = (
        pressure, saturation, permeability, porosity, upwind_flags, diag_inverse, seismic_obs
    )
    scratch = [
        *[pltpu.VMEM(array.shape, array.dtype) for array in large],
        dma((len(large),)),
        pltpu.VMEM((2, 3, 3, nx, ny, nz), f32),
        pltpu.VMEM((2, 3, 3, nx, ny, nz), f32),
        pltpu.VMEM((2, 3, nx, ny, nz), f32),
        pltpu.VMEM((nx, ny, nz), f32),
        pltpu.VMEM((2 * nx * ny, wide), jnp.bfloat16),
        pltpu.VMEM((nz, wide), jnp.bfloat16),
        pltpu.VMEM((8, wide), f32),
        *[pltpu.VMEM(s, f32) for s in bundles],
        *[pltpu.VMEM(s, f32) for s in bundles],
        dma((3, 2)),
        dma((3, 2)),
        pltpu.VMEM((peers, 8, slots), f32),
        pltpu.VMEM((peers, 8, slots), f32),
        dma((peers,)),
        dma((peers,)),
        pltpu.VMEM((n_wells, nz), f32),
        pltpu.VMEM((counts[2], n_wells, nz), f32),
        dma((counts[2],)),
        dma((counts[2],)),
        *[pltpu.VMEM(s, f32) for s in faces],
        *[pltpu.VMEM((2,) + s, f32) for s in faces],
        dma((3, 2)),
        dma((2, 3, 2)),
        pltpu.VMEM((peers, 1, slots), f32),
        pltpu.VMEM((2, peers, 1, slots), f32),
        dma((peers,)),
        dma((2, peers)),
        pltpu.VMEM((counts[0], 2, share), f32),
        pltpu.VMEM((counts[0], 2, share), f32),
        dma((counts[0],)),
        dma((counts[0],)),
        pltpu.VMEM((peers, 2, lanes), f32),
        pltpu.VMEM((peers, 2, lanes), f32),
        dma((peers,)),
        dma((peers,)),
    ]
    return pl.pallas_call(
        functools.partial(kernel, counts),
        out_shape=(
            jax.ShapeDtypeStruct((2, 3, nx, ny, nz), f32),
            jax.ShapeDtypeStruct((2, PARAM_REGIONS), f32),
        ),
        in_specs=[hbm] * 7 + [vmem] * 11,
        out_specs=(vmem, vmem),
        scratch_shapes=scratch,
        compiler_params=pltpu.CompilerParams(
            collective_id=0, has_side_effects=True, vmem_limit_bytes=63 * 2**20
        ),
    )(
        *large,
        well_x,
        well_y,
        well_top,
        well_len,
        well_bhp,
        well_obs,
        fault_cell,
        fault_count,
        fault_trans,
        fault_up,
        region_map,
    )


def solution(mesh):
    placed = (
        P(None, "gx", "gy", "gz"),
        P(None, None, "gx", "gy", "gz"),
        P("gx", "gy", "gz"),
        P("gx", "gy", "gz"),
        P("gx", "gy", "gz"),
        P(None, None, None, "gx", "gy", "gz"),
        P("gx", "gy", "gz"),
        P("gx", "gy", None),
        P("gx", "gy", None),
        P("gx", "gy", None),
        P("gx", "gy", None),
        P(None, "gx", "gy", None),
        P(None, "gx", "gy", None),
        P(("gx", "gy", "gz"), None, None),
        P(("gx", "gy", "gz"), None),
        P(("gx", "gy", "gz"), None, None),
        P(("gx", "gy", "gz"), None, None),
        P("gx", "gy", "gz"),
    )
    return jax.shard_map(
        local,
        mesh=mesh,
        in_specs=placed,
        out_specs=(P(None, None, "gx", "gy", "gz"), P(None, ("gx", "gy", "gz"))),
        check_vma=False,
    )
```
